128 devices in a mesh: tok: 8 (over z, core), lat: 16 (over y, x).
Axes of the slice: x: 4, y: 4, z: 4, core: 2. Of those that a mesh axis runs over, the one named last changes fastest.
Arguments:
- activations: bfloat16 [2048, 2, 8192], P('lat', None, 'tok'), may hold values from -6 to 6
- enc_weight: bfloat16 [64, 2, 8192, 256], P('lat', None, 'tok'), may hold values from -0.046875 to 0.046875
- enc_bias: float32 [64, 256], P('lat'), may hold values from -3 to 3
- dec_weight: bfloat16 [64, 256, 2, 8192], P('lat', None, None, 'tok'), may hold values from -0.09375 to 0.09375
- dec_bias: float32 [2, 8192], P(None, 'tok'), may hold values from -3 to 3
- active: int32 [16, 16], replicated, may hold values from 0 to 63, all different within a row; in each aligned block of 16 rows (0 to 15, 16 to 31, ...) at most 8 rows name the same one
Outputs:
- grad_enc: bfloat16 [64, 2, 8192, 256], P('lat', None, 'tok')
- grad_enc_bias: float32 [64, 256], P('lat')
- grad_dec: bfloat16 [64, 256, 2, 8192], P('lat', None, None, 'tok')
- grad_dec_bias: float32 [2, 8192], P(None, 'tok')
The draws below stay inside these ranges and needn't reach their ends.
Inputs may be any that keep to these rules, and one draw needn't show every extreme that they name: `active`: each row lists 16 different block ids; every block id appears in some row; no block id appears in more than 8 rows, and some block id appears in exactly 8 rows.
All inputs are finite; a program needn't handle non-finite values.
Results may differ from the reference program's by a relative error of at most 0.02.
Values may be sent and summed in bfloat16 or wider, within the bound.
A program may use at most 192 MiB of HBM per device.

```python
import math
import jax
import jax.numpy as jnp
import numpy as np
from jax import lax

D = 8192
MODELS = 2
BLOCK = 256
TOUCH = 4
ACTIVE = 16
MOST = 8
TILE = 128
TILES = 16
NBLK = 64
ROWS = 2048


def shard_levels(stream_key, shape, shards, smallest, high):
    def one(axis_at, blocks):
        heights = jax.random.uniform(jax.random.fold_in(jax.random.fold_in(stream_key, 6), axis_at), (blocks,), jnp.float32, smallest / len(shards), high / len(shards))
        return jnp.repeat(jnp.exp(heights), shape[axis_at] // blocks).reshape((-1,) + (1,) * (len(shape) - axis_at - 1))

    gain = one(*shards[0])
    for cut in shards[1:]:
        gain = gain * one(*cut)
    return gain


def assign_block(stream_key, own, number, rows, count, top, most, lean):
    sequence = jax.random.permutation(stream_key, count)
    heavy_load, usual = load_shares(count, rows * top, most, lean, True), load_shares(count, rows * top, most, lean, False)
    places = jnp.arange(count)

    def named(tallies, offset_by):
        used = int((tallies > 0).sum())
        fixed = max(1, used // 4)
        passed = fixed + (places - fixed + offset_by * (used - fixed)) % max(1, count - fixed)
        return jnp.zeros((count,), jnp.int32).at[sequence[jnp.where(places < fixed, places, passed)]].set(jnp.asarray(tallies, jnp.int32))

    tallies = jnp.where(number % 4 == 0, named(heavy_load, number // 4), named(usual, number - number // 4 - 1))
    mixed = jax.random.permutation(jax.random.fold_in(own, 3), count)
    donor, receiver = mixed[0:count // 2 * 2:2], mixed[1:count // 2 * 2:2]
    margin = jnp.minimum(tallies[donor] - 1, most - tallies[receiver]) // 2
    margin = jnp.where((donor == sequence[0]) | (receiver == sequence[0]) | (tallies[receiver] == 0), 0, jnp.maximum(margin, 0))
    passed = jax.random.randint(jax.random.fold_in(own, 4), (count // 2,), 0, 1 << 20) % (margin + 1)
    tallies = tallies.at[donor].add(-passed).at[receiver].add(passed)
    items = jnp.searchsorted(jnp.cumsum(tallies), jnp.arange(rows * top), side="right").astype(jnp.int32)
    table = items.reshape(top, rows).T
    table = table[jax.random.permutation(jax.random.fold_in(own, 1), rows)]
    offset_by = jax.random.randint(jax.random.fold_in(own, 2), (rows, 1), 0, top)
    return jnp.take_along_axis(table, (jnp.arange(top)[None, :] + offset_by) % top, axis=1)


def load_shares(number_of, total, bound, lean, full):
    portions = [(1 << 20) // math.isqrt(rank ** lean) + 1 for rank in range(1, number_of + 1)]
    largest = bound if full else min(bound, max(-(-total // number_of), total * portions[0] // sum(portions)))
    least = 1 if total - largest >= number_of - 1 else 0
    counts, rest = [largest] + [least] * (number_of - 1), total - largest - least * (number_of - 1)
    while rest > 0:
        movable = [i for i in range(1, number_of) if counts[i] < largest] or [i for i in range(1, number_of) if counts[i] < bound]
        whole, left = sum([portions[i] for i in movable]), rest
        for i in movable:
            extra = min(bound - counts[i], max(1, left * portions[i] // whole), rest)
            counts[i] = counts[i] + extra
            rest = rest - extra
    return np.array(counts)


def gaussian(rng, dims, scale, reach, split=(), kind=jnp.bfloat16):
    level = shard_levels(rng, dims, split, -0.22, 0.18) if split else 1.0
    result = jax.random.normal(rng, dims, jnp.float32) * scale * level
    return jnp.minimum(jnp.maximum(result, -reach), reach).astype(kind)


def setup_inputs(seed: int = 0) -> dict:
    splits = jax.random.split(jax.random.key(seed), 7)
    activations = gaussian(splits[0], (ROWS, MODELS, D), 1.0, 6.0, ((0, 16), (2, 8)))
    enc_weight = gaussian(splits[1], (NBLK, MODELS, D, BLOCK), (MODELS * D) ** -0.5, 0.046875, ((0, 16), (2, 8)))
    enc_bias = gaussian(splits[2], (NBLK, BLOCK), 0.5, 3.0, ((0, 16),), jnp.float32)
    dec_weight = gaussian(splits[3], (NBLK, BLOCK, MODELS, D), (ACTIVE * BLOCK) ** -0.5, 0.09375, ((0, 16), (3, 8)))
    dec_bias = gaussian(splits[4], (MODELS, D), 0.5, 3.0, ((1, 8),), jnp.float32)
    active_keys = jax.random.split(jax.random.fold_in(splits[5], 1), TILES // TILES)
    active_turns = jax.random.permutation(jax.random.fold_in(splits[5], 3), TILES // TILES)
    active = jax.vmap(lambda own, number: assign_block(jax.random.fold_in(splits[5], 2), own, number, TILES, NBLK, ACTIVE, MOST, 1))(active_keys, active_turns).reshape((TILES, ACTIVE))
    return {"activations": activations, "enc_weight": enc_weight, "enc_bias": enc_bias, "dec_weight": dec_weight, "dec_bias": dec_bias, "active": active}


SPARSITY = 0.25
NORM_EPSILON = 1e-06

def slot_lists(active, first_block, block_count):
    tile_count = active.shape[0]
    block_ids = first_block + jnp.arange(block_count, dtype=jnp.int32)
    is_active = jnp.any(active[:, :, None] == block_ids[None, None, :], axis=1).astype(jnp.int32)
    rank_count = jnp.cumsum(is_active, axis=0).astype(jnp.int32)
    wanted = jnp.arange(MOST, dtype=jnp.int32) + 1
    picked = (is_active[:, :, None] == 1) & (rank_count[:, :, None] == wanted[None, None, :])
    tile_ids = jnp.arange(tile_count, dtype=jnp.int32)
    slot_tile = lax.optimization_barrier(jnp.sum(jnp.where(picked, tile_ids[:, None, None], 0), axis=0)).astype(jnp.int32)
    live_slot = jnp.any(picked, axis=0)
    return (slot_tile, live_slot)

def reference(activations, enc_weight, enc_bias, dec_weight, dec_bias, active):
    tile_count = active.shape[0]
    loss_scale = 1.0 / math.sqrt(MOST * TILE)
    tile_acts = activations.reshape(tile_count, TILE, MODELS, D)

    def forward(recon_sum, owner_index):
        first_block = owner_index * TOUCH
        slot_tile, live_slot = slot_lists(active, first_block, TOUCH)
        enc_slab = lax.dynamic_slice_in_dim(enc_weight, first_block, TOUCH, 0)
        bias_slab = lax.dynamic_slice_in_dim(enc_bias, first_block, TOUCH, 0)
        dec_slab = lax.dynamic_slice_in_dim(dec_weight, first_block, TOUCH, 0)
        partial_value = jnp.zeros((tile_count, TILE, MODELS, D), jnp.float32)
        feature_list = []
        for slab_index in range(TOUCH):
            chosen = tile_acts[slot_tile[slab_index]].astype(jnp.float32)
            pre_act = jnp.einsum('mrad,adj->mrj', chosen, enc_slab[slab_index].astype(jnp.float32))
            pre_act = pre_act + bias_slab[slab_index][None, None, :]
            features = jnp.where(live_slot[slab_index][:, None, None], jnp.maximum(pre_act, 0.0), 0.0).astype(jnp.bfloat16)
            product = jnp.einsum('mrj,jad->mrad', features.astype(jnp.float32), dec_slab[slab_index].astype(jnp.float32))
            partial_value = partial_value.at[slot_tile[slab_index]].add(product)
            feature_list.append(features)
        rounded = lax.optimization_barrier(partial_value.astype(jnp.bfloat16)).astype(jnp.float32)
        return (recon_sum + rounded, jnp.stack(feature_list))
    owners = jnp.arange(tile_count, dtype=jnp.int32)
    recon_sum, all_features = lax.scan(forward, jnp.zeros((tile_count, TILE, MODELS, D), jnp.float32), owners)
    recon = recon_sum + dec_bias[None, None, :, :]
    error = (recon - tile_acts.astype(jnp.float32)).astype(jnp.bfloat16)

    def backward(owner_index):
        first_block = owner_index * TOUCH
        slot_tile, live_slot = slot_lists(active, first_block, TOUCH)
        dec_slab = lax.dynamic_slice_in_dim(dec_weight, first_block, TOUCH, 0)
        owner_features = all_features[owner_index]
        dec_norms = jnp.sqrt(lax.optimization_barrier(jnp.sum(jnp.square(dec_slab.astype(jnp.float32)), axis=3)) + NORM_EPSILON)
        enc_grads = []
        bias_grads = []
        dec_grads = []
        for slab_index in range(TOUCH):
            features = owner_features[slab_index]
            chosen = tile_acts[slot_tile[slab_index]].astype(jnp.float32)
            err_chosen = error[slot_tile[slab_index]].astype(jnp.float32)
            dec_wide = dec_slab[slab_index].astype(jnp.float32)
            grad_sum = jnp.einsum('mrad,jad->mrj', err_chosen, dec_wide)
            feat_grad = loss_scale * (grad_sum + SPARSITY * lax.optimization_barrier(jnp.sum(dec_norms[slab_index], axis=1))[None, None, :])
            pre_grad = jnp.where(features > 0, feat_grad, 0.0).astype(jnp.bfloat16)
            pre_wide = pre_grad.astype(jnp.float32)
            enc_grads.append(jnp.einsum('mrad,mrj->adj', chosen, pre_wide).astype(jnp.bfloat16))
            bias_grads.append(lax.optimization_barrier(jnp.sum(pre_wide, axis=(0, 1))))
            feat_wide = features.astype(jnp.float32)
            feat_total = lax.optimization_barrier(jnp.sum(feat_wide, axis=(0, 1)))
            recon_term = jnp.einsum('mrj,mrad->jad', feat_wide, err_chosen)
            norm_term = SPARSITY * feat_total[:, None, None] * dec_wide / dec_norms[slab_index][:, :, None]
            dec_grads.append((loss_scale * (recon_term + norm_term)).astype(jnp.bfloat16))
        return (jnp.stack(enc_grads), jnp.stack(bias_grads), jnp.stack(dec_grads))
    enc_grads, bias_grads, dec_grads = lax.map(backward, owners)
    grad_enc = enc_grads.reshape(NBLK, MODELS, D, BLOCK)
    grad_enc_bias = bias_grads.reshape(NBLK, BLOCK)
    grad_dec = dec_grads.reshape(NBLK, BLOCK, MODELS, D)
    grad_dec_bias = loss_scale * lax.optimization_barrier(jnp.sum(error.astype(jnp.float32), axis=(0, 1)))
    return (grad_enc, grad_enc_bias, grad_dec, grad_dec_bias)
```

```python
import functools
import math

import jax
import jax.numpy as jnp
from jax import lax
from jax.experimental import pallas as pl
from jax.experimental.pallas import tpu as pltpu
from jax.sharding import PartitionSpec as P

MOST = 8
TILE = 128
SPARSITY = 0.25
NORM_EPSILON = 1e-06
DEAD = -1e30
MESH = pl.DeviceIdType.MESH
SIDE = 4
BIG = 56 * 1024 * 1024
DIRS = (1, -1)


def params(**kw):
    return pltpu.CompilerParams(vmem_limit_bytes=BIG, **kw)


def ring(i, step):
    return lax.rem(i + step + SIDE, SIDE)


def lat_peer(y, x):
    return {"lat": y * SIDE + x}


def plane():
    lat = lax.axis_index("lat")
    return lax.rem(lat, SIDE), lax.div(lat, SIDE)


def greet(peers):
    barrier = pltpu.get_barrier_semaphore()
    for peer in peers:
        pl.semaphore_signal(barrier, inc=1, device_id=peer, device_id_type=MESH)
    pl.semaphore_wait(barrier, len(peers))


def greet_plane():
    x, y = plane()
    greet(
        [lat_peer(y, ring(x, d)) for d in DIRS] + [lat_peer(ring(y, d), x) for d in DIRS]
    )


def remote(src, dst, send, recv, peer):
    return pltpu.make_async_remote_copy(
        src_ref=src, dst_ref=dst, send_sem=send, recv_sem=recv, device_id=peer, device_id_type=MESH
    )


def half_rows(d, rows):
    return pl.ds(0 if d == 1 else rows // 2, rows // 2)


class Plane:
    def __init__(self, h):
        x, y = plane()
        self.h = h
        self.p, self.q = (x, y) if h == 0 else (y, x)

    def tile(self, p, q):
        return q * SIDE + p if self.h == 0 else p * SIDE + q

    def near(self, dp, dq):
        p, q = ring(self.p, dp), ring(self.q, dq)
        return lat_peer(q, p) if self.h == 0 else lat_peer(p, q)


def gather_plane(own, out, send, recv):
    rows = out.shape[2]
    flows = [Plane(h) for h in (0, 1)]
    started = []

    def go(copy):
        copy.start()
        started.append(copy)

    def sems(h, phase, k, d):
        n = ((h * 2 + phase) * SIDE + k) * 2 + (0 if d == 1 else 1)
        return n

    def first_full(f, d):
        n = sems(f.h, 0, 0, d)
        return remote(
            own(f.h), out.at[f.tile(f.p, f.q), f.h], send.at[n], recv.at[n], f.near(d, 0)
        )

    def first_half(f, d):
        n = sems(f.h, 0, 1, d)
        at = out.at[f.tile(ring(f.p, -d), f.q), f.h, half_rows(d, rows)]
        return remote(at, at, send.at[n], recv.at[n], f.near(d, 0))

    def second_full(f, k, d):
        n = sems(f.h, 1, k, d)
        at = out.at[f.tile(ring(f.p, -k), f.q), f.h]
        return remote(own(f.h) if k == 0 else at, at, send.at[n], recv.at[n], f.near(0, d))

    def second_half(f, k, d):
        n = 32 + ((f.h * SIDE) + k) * 2 + (0 if d == 1 else 1)
        at = out.at[f.tile(ring(f.p, -k), ring(f.q, -d)), f.h, half_rows(d, rows)]
        return remote(at, at, send.at[n], recv.at[n], f.near(0, d))

    for f in flows:
        for d in DIRS:
            go(first_full(f, d))
    for f in flows:
        for d in DIRS:
            go(second_full(f, 0, d))
    for f in flows:
        for d, k in ((1, 1), (-1, 3)):
            first_full(f, d).wait_recv()
            go(first_half(f, d))
            for e in DIRS:
                go(second_full(f, k, e))
    for f in flows:
        for d in DIRS:
            second_full(f, 0, d).wait_recv()
            go(second_half(f, 0, d))
    for f in flows:
        for d in DIRS:
            first_half(f, d).wait_recv()
        for e in DIRS:
            go(second_full(f, 2, e))
    for k in (1, 3, 2):
        for f in flows:
            for d in DIRS:
                second_full(f, k, d).wait_recv()
                go(second_half(f, k, d))
    for k in range(SIDE):
        for f in flows:
            for d in DIRS:
                second_half(f, k, d).wait_recv()
    for copy in started:
        copy.wait_send()


def gather_kernel(x_ref, out_ref, local, send, recv):
    greet_plane()
    x, y = plane()
    keep = pltpu.make_async_copy(x_ref, out_ref.at[y * SIDE + x], local)
    keep.start()
    gather_plane(lambda h: x_ref.at[h], out_ref, send, recv)
    keep.wait()


def gather_acts(mine):
    any_space = pl.BlockSpec(memory_space=pl.ANY)
    return pl.pallas_call(
        gather_kernel,
        out_shape=jax.ShapeDtypeStruct((SIDE * SIDE,) + mine.shape, mine.dtype),
        in_specs=[any_space],
        out_specs=any_space,
        scratch_shapes=[
            pltpu.SemaphoreType.DMA,
            pltpu.SemaphoreType.DMA((48,)),
            pltpu.SemaphoreType.DMA((48,)),
        ],
        compiler_params=params(collective_id=0, has_side_effects=True),
        name="gather_acts",
    )(mine)


CHUNK = 32


def by_rows(rows, body):
    def step(i, carry):
        body(pl.multiple_of(i * CHUNK, CHUNK))
        return carry

    lax.fori_loop(0, rows // CHUNK, step, 0)


def f32(v):
    return v.astype(jnp.float32)


def recon_kernel(
    part, act, bias, out, r1, r2, s2, c, r4, r5, s5, err, local, send, recv, gsend, grecv
):
    greet_plane()
    rows = part.shape[2]
    half = rows // 2
    flows = [Plane(h) for h in (0, 1)]
    started = []

    def go(copy):
        copy.start()
        started.append(copy)

    def s(d):
        return 0 if d == 1 else 1

    def num(kind, h, j, d):
        return ((kind * 2 + h) * SIDE + j) * 2 + s(d)

    def far(f, j, d):
        n = num(0, f.h, j, d)
        t = f.tile(ring(f.p, 2), ring(f.q, j))
        return remote(
            part.at[t, f.h, half_rows(d, rows)], r1.at[f.h, j, s(d)], send.at[n], recv.at[n], f.near(d, 0)
        )

    def plain(f, j, d):
        n = num(1, f.h, j, d)
        t = f.tile(ring(f.p, d), ring(f.q, j))
        return remote(
            part.at[t, f.h, half_rows(-d, rows)],
            r2.at[f.h, j, s(d), half_rows(-d, rows)],
            send.at[n],
            recv.at[n],
            f.near(d, 0),
        )

    def summed(f, j, d):
        n = num(2, f.h, j, d)
        return remote(
            s2.at[f.h, j, s(d)],
            r2.at[f.h, j, s(d), half_rows(d, rows)],
            send.at[n],
            recv.at[n],
            f.near(d, 0),
        )

    def far2(f, d):
        n = num(3, f.h, 0, d)
        return remote(
            c.at[f.h, 2, half_rows(d, rows)], r4.at[f.h, s(d)], send.at[n], recv.at[n], f.near(0, d)
        )

    def plain2(f, d):
        n = num(3, f.h, 1, d)
        return remote(
            c.at[f.h, 1 if d == 1 else 3, half_rows(-d, rows)],
            r5.at[f.h, s(d), half_rows(-d, rows)],
            send.at[n],
            recv.at[n],
            f.near(0, d),
        )

    def summed2(f, d):
        n = num(3, f.h, 2, d)
        return remote(
            s5.at[f.h, s(d)], r5.at[f.h, s(d), half_rows(d, rows)], send.at[n], recv.at[n], f.near(0, d)
        )

    order = (2, 1, 3, 0)
    for j in order:
        for f in flows:
            for d in DIRS:
                go(far(f, j, d))
        for f in flows:
            for d in DIRS:
                go(plain(f, j, d))

    def add_far(f, j):
        for d in DIRS:
            far(f, j, d).wait_recv()
            t = f.tile(ring(f.p, d), ring(f.q, j))
            base = 0 if d == 1 else half

            def add(i, t=t, base=base, d=d):
                s2[f.h, j, s(d), pl.ds(i, CHUNK)] = (
                    f32(part[t, f.h, pl.ds(base + i, CHUNK)]) + f32(r1[f.h, j, s(d), pl.ds(i, CHUNK)])
                ).astype(jnp.bfloat16)

            by_rows(half, add)
            go(summed(f, j, d))

    def reduce(f, j):
        for d in DIRS:
            plain(f, j, d).wait_recv()
            summed(f, j, d).wait_recv()
        t = f.tile(f.p, ring(f.q, j))

        def add(i):
            at = pl.ds(i, CHUNK)
            c[f.h, j, at] = (
                f32(part[t, f.h, at]) + f32(r2[f.h, j, 0, at]) + f32(r2[f.h, j, 1, at])
            ).astype(jnp.bfloat16)

        by_rows(rows, add)

    for j in order:
        for f in flows:
            add_far(f, j)
    for f in flows:
        reduce(f, 2)
        for d in DIRS:
            go(far2(f, d))
    for f in flows:
        for d, j in ((1, 1), (-1, 3)):
            reduce(f, j)
            go(plain2(f, d))
    for f in flows:
        for d, j in ((1, 1), (-1, 3)):
            far2(f, d).wait_recv()
            base = 0 if d == 1 else half

            def add(i, j=j, base=base, d=d):
                s5[f.h, s(d), pl.ds(i, CHUNK)] = (
                    f32(c[f.h, j, pl.ds(base + i, CHUNK)]) + f32(r4[f.h, s(d), pl.ds(i, CHUNK)])
                ).astype(jnp.bfloat16)

            by_rows(half, add)
            go(summed2(f, d))
    for f in flows:
        reduce(f, 0)
    for f in flows:
        for d in DIRS:
            plain2(f, d).wait_recv()
            summed2(f, d).wait_recv()

        def add(i):
            at = pl.ds(i, CHUNK)
            recon = f32(c[f.h, 0, at]) + f32(r5[f.h, 0, at]) + f32(r5[f.h, 1, at]) + bias[f.h][None, :]
            err[f.h, at] = (recon - f32(act[f.h, at])).astype(jnp.bfloat16)

        by_rows(rows, add)
    for copy in started:
        copy.wait_send()
    x, y = plane()
    keep = pltpu.make_async_copy(err, out.at[y * SIDE + x], local)
    keep.start()
    gather_plane(lambda h: err.at[h], out, gsend, grecv)
    keep.wait()


def recon_error(part, act, bias):
    tiles, models, rows, width = part.shape
    half = rows // 2
    vmem = pl.BlockSpec(memory_space=pltpu.VMEM)
    b = jnp.bfloat16
    return pl.pallas_call(
        recon_kernel,
        out_shape=jax.ShapeDtypeStruct(part.shape, part.dtype),
        in_specs=[vmem] * 3,
        out_specs=pl.BlockSpec(memory_space=pl.ANY),
        scratch_shapes=[
            pltpu.VMEM((2, SIDE, 2, half, width), b),
            pltpu.VMEM((2, SIDE, 2, rows, width), b),
            pltpu.VMEM((2, SIDE, 2, half, width), b),
            pltpu.VMEM((2, SIDE, rows, width), b),
            pltpu.VMEM((2, 2, half, width), b),
            pltpu.VMEM((2, 2, rows, width), b),
            pltpu.VMEM((2, 2, half, width), b),
            pltpu.VMEM((2, rows, width), b),
            pltpu.SemaphoreType.DMA,
            pltpu.SemaphoreType.DMA((64,)),
            pltpu.SemaphoreType.DMA((64,)),
            pltpu.SemaphoreType.DMA((48,)),
            pltpu.SemaphoreType.DMA((48,)),
        ],
        compiler_params=params(collective_id=1, has_side_effects=True),
        name="recon_error",
    )(part, act, bias)


def tok_peer(z, core):
    return {"tok": z * 2 + core}


def tok_sum_kernel(epilogue, n_extra, part, *refs):
    extra, (out, r1, s1, r2, r3, s3, own, local, send, recv) = refs[:n_extra], refs[n_extra:]
    tok = lax.axis_index("tok")
    z, core = lax.div(tok, 2), lax.rem(tok, 2)
    other = tok_peer(z, 1 - core)
    greet([other] + [tok_peer(ring(z, d), core) for d in DIRS])
    group = part.shape[1] // 2
    half = group // 2
    mine, theirs = pl.ds(core * group, group), pl.ds((1 - core) * group, group)
    started = []

    def go(copy):
        copy.start()
        started.append(copy)

    def s(d):
        return 0 if d == 1 else 1

    def hs(d):
        return pl.ds(0 if d == 1 else half, half)

    def swap(j):
        at = ring(z, j)
        return remote(part.at[at, theirs], r1.at[j], send.at[j], recv.at[j], other)

    def far(d):
        n = 4 + s(d)
        return remote(s1.at[2, hs(d)], r2.at[s(d)], send.at[n], recv.at[n], tok_peer(ring(z, d), core))

    def plain(d):
        n = 6 + s(d)
        return remote(
            s1.at[1 if d == 1 else 3, hs(-d)],
            r3.at[s(d), hs(-d)],
            send.at[n],
            recv.at[n],
            tok_peer(ring(z, d), core),
        )

    def summed(d):
        n = 8 + s(d)
        return remote(
            s3.at[s(d)], r3.at[s(d), hs(d)], send.at[n], recv.at[n], tok_peer(ring(z, d), core)
        )

    def spread(d):
        n = 10 + s(d)
        return remote(own, out.at[z, mine], send.at[n], recv.at[n], tok_peer(ring(z, d), core))

    def forward(d):
        n = 12 + s(d)
        at = out.at[ring(z, -d), pl.ds(core * group + (0 if d == 1 else half), half)]
        return remote(at, at, send.at[n], recv.at[n], tok_peer(ring(z, d), core))

    def hand(j):
        n = 14 + j
        at = out.at[ring(z, j), mine]
        return remote(own if j == 0 else at, at, send.at[n], recv.at[n], other)

    order = (2, 1, 3, 0)
    for j in order:
        go(swap(j))

    def first(j):
        swap(j).wait_recv()
        at = ring(z, j)

        def add(i, carry):
            s1[j, i] = (f32(part[at, core * group + i]) + f32(r1[j, i])).astype(s1.dtype)
            return carry

        lax.fori_loop(0, group, add, 0)

    first(2)
    for d in DIRS:
        go(far(d))
    for d in DIRS:
        first(1 if d == 1 else 3)
        go(plain(d))
    first(0)
    for d in DIRS:
        far(d).wait_recv()
        j, base = (1, 0) if d == 1 else (3, half)

        def add(i, carry, j=j, base=base, d=d):
            s3[s(d), i] = (f32(s1[j, base + i]) + f32(r2[s(d), i])).astype(s3.dtype)
            return carry

        lax.fori_loop(0, half, add, 0)
        go(summed(d))
    for d in DIRS:
        plain(d).wait_recv()
        summed(d).wait_recv()

    def last(i, carry):
        total = f32(s1[0, i]) + f32(r3[0, i]) + f32(r3[1, i])
        own[i] = epilogue(total, z, core * group + i, *extra).astype(own.dtype)
        return carry

    lax.fori_loop(0, group, last, 0)
    keep = pltpu.make_async_copy(own, out.at[z, mine], local)
    keep.start()
    for d in DIRS:
        go(spread(d))
    go(hand(0))
    for d in DIRS:
        spread(d).wait_recv()
        go(forward(d))
        go(hand(3 if d == 1 else 1))
    for d in DIRS:
        forward(d).wait_recv()
    go(hand(2))
    for j in range(SIDE):
        hand(j).wait_recv()
    for copy in started:
        copy.wait_send()
    keep.wait()


def tok_sum(name, collective_id, epilogue, part, *extra):
    slabs, slots, rows, width = part.shape
    group = slots // 2
    vmem = pl.BlockSpec(memory_space=pltpu.VMEM)
    t, b = part.dtype, jnp.bfloat16
    return pl.pallas_call(
        functools.partial(tok_sum_kernel, epilogue, len(extra)),
        out_shape=jax.ShapeDtypeStruct(part.shape, b),
        in_specs=[vmem] * (1 + len(extra)),
        out_specs=pl.BlockSpec(memory_space=pl.ANY),
        scratch_shapes=[
            pltpu.VMEM((SIDE, group, rows, width), t),
            pltpu.VMEM((SIDE, group, rows, width), t),
            pltpu.VMEM((2, group // 2, rows, width), t),
            pltpu.VMEM((2, group, rows, width), t),
            pltpu.VMEM((2, group // 2, rows, width), t),
            pltpu.VMEM((group, rows, width), b),
            pltpu.SemaphoreType.DMA,
            pltpu.SemaphoreType.DMA((18,)),
            pltpu.SemaphoreType.DMA((18,)),
        ],
        compiler_params=params(collective_id=collective_id, has_side_effects=True),
        name=name,
    )(part, *extra)


def encode_kernel(tile_of, live, acts, enc, out):
    slab = pl.program_id(0)
    for r in range(0, MOST, 2):
        at = slab * MOST + r

        @pl.when(live[at] == 1)
        def _():
            total = None
            for m in range(acts.shape[1]):
                x = jnp.concatenate([acts[tile_of[at], m], acts[tile_of[at + 1], m]], axis=0)
                term = jnp.dot(x, enc[0, m], preferred_element_type=jnp.float32)
                total = term if total is None else total + term
            out[0, r] = total[:TILE]
            out[0, r + 1] = jnp.where(live[at + 1] == 1, total[TILE:], DEAD)

        @pl.when(live[at] == 0)
        def _():
            out[0, r] = jnp.full(out.shape[2:], DEAD, out.dtype)
            out[0, r + 1] = jnp.full(out.shape[2:], DEAD, out.dtype)


def whole(shape):
    return pl.BlockSpec(shape, lambda *_: (0,) * len(shape))


def slabwise(shape):
    return pl.BlockSpec((1,) + shape[1:], lambda s, *_: (s,) + (0,) * (len(shape) - 1))


def slab_call(kernel, name, lists, ins, outs, scratch=()):
    return pl.pallas_call(
        kernel,
        out_shape=[jax.ShapeDtypeStruct(s, t) for s, t in outs],
        grid_spec=pltpu.PrefetchScalarGridSpec(
            num_scalar_prefetch=len(lists),
            grid=(SIDE,),
            in_specs=[spec(a.shape) for a, spec in ins],
            out_specs=[slabwise(s) for s, _ in outs],
            scratch_shapes=list(scratch),
        ),
        compiler_params=params(),
        name=name,
    )(*lists, *[a for a, _ in ins])


def decode_kernel(rank, feat, dec, out, acc):
    tile = pl.program_id(0)
    acc[...] = jnp.zeros_like(acc)
    for s in range(dec.shape[0]):
        r = rank[tile * dec.shape[0] + s]

        @pl.when(r >= 0)
        def _():
            f = feat[s, r]
            for m in range(dec.shape[1]):
                acc[m] += jnp.dot(f, dec[s, m], preferred_element_type=jnp.float32)

    out[0] = acc[...].astype(out.dtype)


def decode(rank, feat, dec):
    tiles = SIDE * SIDE
    models, width = dec.shape[1], dec.shape[3]
    shape = (tiles, models, TILE, width)
    return pl.pallas_call(
        decode_kernel,
        out_shape=jax.ShapeDtypeStruct(shape, jnp.bfloat16),
        grid_spec=pltpu.PrefetchScalarGridSpec(
            num_scalar_prefetch=1,
            grid=(tiles,),
            in_specs=[whole(feat.shape), whole(dec.shape)],
            out_specs=slabwise(shape),
            scratch_shapes=[pltpu.VMEM(shape[1:], jnp.float32)],
        ),
        compiler_params=params(),
        name="decode",
    )(rank, feat, dec)


NT = (((1,), (1,)), ((), ()))
TN = (((0,), (0,)), ((), ()))


def dec_grad_kernel(scale, tile_of, live, err, dec, feat, inv_norm, part, grad_dec, acc, tot):
    slab = pl.program_id(0)
    acc[...] = jnp.zeros_like(acc)
    tot[...] = jnp.zeros_like(tot)
    for r in range(0, MOST, 2):
        at = slab * MOST + r

        @pl.when(live[at] == 1)
        def _():
            f = jnp.concatenate([feat[0, r], feat[0, r + 1]], axis=0)
            total = None
            for m in range(err.shape[1]):
                e = jnp.concatenate([err[tile_of[at], m], err[tile_of[at + 1], m]], axis=0)
                term = lax.dot_general(e, dec[0, m], NT, preferred_element_type=jnp.float32)
                total = term if total is None else total + term
                acc[m] += lax.dot_general(f, e, TN, preferred_element_type=jnp.float32)
            part[0, r] = total[:TILE].astype(part.dtype)
            part[0, r + 1] = total[TILE:].astype(part.dtype)
            ones = jnp.ones((2 * TILE, 128), jnp.bfloat16)
            tot[...] += lax.dot_general(f, ones, TN, preferred_element_type=jnp.float32)

        @pl.when(live[at] == 0)
        def _():
            part[0, r] = jnp.zeros(part.shape[2:], part.dtype)
            part[0, r + 1] = jnp.zeros(part.shape[2:], part.dtype)

    for m in range(err.shape[1]):
        col = SPARSITY * tot[:, :1] * inv_norm[0, m]
        grad_dec[0, m] = (scale * (acc[m] + col * f32(dec[0, m]))).astype(grad_dec.dtype)


def enc_grad_kernel(tile_of, live, acts, pre_grad, grad_enc, grad_bias, acc):
    slab = pl.program_id(0)
    acc[...] = jnp.zeros_like(acc)
    grad_bias[...] = jnp.sum(f32(pre_grad[0]), axis=(0, 1))[None, None, :]
    for r in range(0, MOST, 2):
        at = slab * MOST + r

        @pl.when(live[at] == 1)
        def _():
            g = jnp.concatenate([pre_grad[0, r], pre_grad[0, r + 1]], axis=0)
            for m in range(acts.shape[1]):
                x = jnp.concatenate([acts[tile_of[at], m], acts[tile_of[at + 1], m]], axis=0)
                acc[m] += lax.dot_general(x, g, TN, preferred_element_type=jnp.float32)

    grad_enc[0] = acc[...].astype(grad_enc.dtype)


def slot_lists(active, first_block, block_count):
    tile_count = active.shape[0]
    block_ids = first_block + jnp.arange(block_count, dtype=jnp.int32)
    is_active = jnp.any(active[:, :, None] == block_ids[None, None, :], axis=1).astype(jnp.int32)
    upto = (jnp.arange(tile_count)[:, None] >= jnp.arange(tile_count)[None, :]).astype(jnp.int32)
    rank_count = jnp.sum(upto[:, :, None] * is_active[None, :, :], axis=1)
    wanted = jnp.arange(MOST, dtype=jnp.int32) + 1
    picked = (is_active[:, :, None] == 1) & (rank_count[:, :, None] == wanted[None, None, :])
    tile_ids = jnp.arange(tile_count, dtype=jnp.int32)
    slot_tile = jnp.sum(jnp.where(picked, tile_ids[:, None, None], 0), axis=0)
    live_slot = jnp.any(picked, axis=0).astype(jnp.int32)
    rank = jnp.where(is_active == 1, rank_count - 1, -1)
    return slot_tile.reshape(-1), live_slot.reshape(-1), rank.reshape(-1)


def feature_of(total, z, slot, bias):
    return jnp.maximum(total + bias[z], 0.0)


def pre_grad_of(scale, total, z, slot, feat, norm):
    grad = scale * (total + SPARSITY * norm[z])
    return jnp.where(f32(feat[z, slot]) > 0.0, grad, 0.0)


def on_device(activations, enc_weight, enc_bias, dec_weight, dec_bias, active):
    slabs = enc_weight.shape[0]
    scale = 1.0 / math.sqrt(MOST * TILE)
    width = activations.shape[2]
    block = enc_weight.shape[3]
    slot_tile, live, rank = slot_lists(active, lax.axis_index("lat") * slabs, slabs)
    mine = activations.transpose(1, 0, 2)
    dec = dec_weight.transpose(0, 2, 1, 3)
    squares = lax.psum(jnp.sum(jnp.square(dec.astype(jnp.float32)), axis=3), "tok")
    norms = jnp.sqrt(squares + NORM_EPSILON)
    acts = gather_acts(mine)
    pre_shape = (slabs, MOST, TILE, block)
    (pre,) = slab_call(
        encode_kernel,
        "encode",
        (slot_tile, live),
        [(acts, whole), (enc_weight, slabwise)],
        [(pre_shape, jnp.float32)],
    )
    feat = tok_sum("features", 2, feature_of, pre, enc_bias.reshape(slabs, 1, block))
    part = decode(rank, feat, dec)
    err = recon_error(part, mine, dec_bias)
    grad_part, grad_dec = slab_call(
        functools.partial(dec_grad_kernel, scale),
        "dec_grad",
        (slot_tile, live),
        [(err, whole), (dec, slabwise), (feat, slabwise), ((1.0 / norms)[..., None], slabwise)],
        [(pre_shape, jnp.bfloat16), (dec.shape, jnp.bfloat16)],
        [pltpu.VMEM(dec.shape[1:], jnp.float32), pltpu.VMEM((block, 128), jnp.float32)],
    )
    pre_grad = tok_sum(
        "pre_grad",
        3,
        functools.partial(pre_grad_of, scale),
        grad_part,
        feat,
        jnp.sum(norms, axis=1).reshape(slabs, 1, block),
    )
    grad_enc, grad_enc_bias = slab_call(
        enc_grad_kernel,
        "enc_grad",
        (slot_tile, live),
        [(acts, whole), (pre_grad, slabwise)],
        [(enc_weight.shape, jnp.bfloat16), ((slabs, 1, block), jnp.float32)],
        [pltpu.VMEM(enc_weight.shape[1:], jnp.float32)],
    )
    grad_dec_bias = scale * jnp.sum(err.astype(jnp.float32), axis=(0, 2))
    return (
        grad_enc,
        grad_enc_bias.reshape(slabs, block),
        grad_dec.transpose(0, 2, 1, 3),
        grad_dec_bias,
    )


def solution(mesh):
    placed = (
        P("lat", None, "tok"),
        P("lat", None, "tok", None),
        P("lat", None),
        P("lat", None, None, "tok"),
        P(None, "tok"),
        P(),
    )
    return jax.shard_map(
        on_device,
        mesh=mesh,
        in_specs=placed,
        out_specs=(
            P("lat", None, "tok", None),
            P("lat", None),
            P("lat", None, None, "tok"),
            P(None, "tok"),
        ),
        check_vma=False,
    )
```

```python
import functools
import math

import jax
import jax.numpy as jnp
from jax import lax
from jax.experimental import pallas as pl
from jax.experimental.pallas import tpu as pltpu
from jax.sharding import PartitionSpec as P

MOST = 8
TILE = 128
SPARSITY = 0.25
NORM_EPSILON = 1e-06
MESH = pl.DeviceIdType.MESH
SIDE = 4
UNIT = TILE // 2
HALF = UNIT // 2
CHUNK = 32
DIRS = (1, -1)
ORDER = (0, 1, 3, 2)
BF16, F32 = jnp.bfloat16, jnp.float32
NT = (((1,), (1,)), ((), ()))
TN = (((0,), (0,)), ((), ()))


def ring(i, step):
    return lax.rem(i + step + SIDE, SIDE)


def lat_peer(y, x):
    return {"lat": y * SIDE + x}


def tok_peer(z, core):
    return {"tok": z * 2 + core}


def plane():
    lat = lax.axis_index("lat")
    return lax.rem(lat, SIDE), lax.div(lat, SIDE)


def column():
    tok = lax.axis_index("tok")
    return lax.div(tok, 2), lax.rem(tok, 2)


def greet():
    x, y = plane()
    z, core = column()
    peers = [lat_peer(y, ring(x, d)) for d in DIRS] + [lat_peer(ring(y, d), x) for d in DIRS]
    peers += [tok_peer(ring(z, d), core) for d in DIRS] + [tok_peer(z, 1 - core)]
    barrier = pltpu.get_barrier_semaphore()
    for peer in peers:
        pl.semaphore_signal(barrier, inc=1, device_id=peer, device_id_type=MESH)
    pl.semaphore_wait(barrier, len(peers))


def s(d):
    return 0 if d == 1 else 1


def rows_of(d):
    return pl.ds(0 if d == 1 else HALF, HALF)


def f32(v):
    return v.astype(F32)


class Wires:
    def __init__(self, send, recv):
        self.send, self.recv = send, recv
        self.numbers, self.started = {}, []

    def copy(self, key, src, dst, peer):
        n = self.numbers.setdefault(key, len(self.numbers))
        return pltpu.make_async_remote_copy(
            src_ref=src,
            dst_ref=dst,
            send_sem=self.send.at[n],
            recv_sem=self.recv.at[n],
            device_id=peer,
            device_id_type=MESH,
        )

    def go(self, copy):
        copy.start()
        self.started.append(copy)

    def drain(self):
        for copy in self.started:
            copy.wait_send()


class Flow:
    def __init__(self, h):
        x, y = plane()
        self.h = h
        self.p, self.q = (x, y) if h == 0 else (y, x)

    def near(self, dp, dq):
        p, q = ring(self.p, dp), ring(self.q, dq)
        return lat_peer(q, p) if self.h == 0 else lat_peer(p, q)

    def unit(self, dq):
        return self.h * SIDE + ring(self.q, dq)


FLOWS = (0, 1)


def sweep(wires, tag, own, held, arrived, flow):
    flows = [Flow(h) for h in FLOWS]

    def p1(f, d):
        dst = held.at[1 if d == 1 else 3, f.unit(0)]
        return wires.copy((tag, 0, f.h, d), own(f.h), dst, f.near(d, 0))

    def p1half(f, d):
        src = held.at[1 if d == 1 else 3, f.unit(0), rows_of(d)]
        return wires.copy((tag, 1, f.h, d), src, held.at[2, f.unit(0), rows_of(d)], f.near(d, 0))

    def p2(f, k, d):
        at = held.at[k, f.unit(0)]
        return wires.copy((tag, 2, f.h, k, d), own(f.h) if k == 0 else at, at, f.near(0, d))

    def p2half(f, k, d):
        at = held.at[k, f.unit(-d), rows_of(d)]
        return wires.copy((tag, 3, f.h, k, d), at, at, f.near(0, d))

    def each(make, *k):
        for f in flows:
            for d in DIRS:
                wires.go(make(f, *k, d))

    def relay(k):
        for f in flows:
            for d in DIRS:
                p2(f, k, d).wait_recv()
                wires.go(p2half(f, k, d))

    def complete(k):
        for f in flows:
            for d in DIRS:
                p2half(f, k, d).wait_recv()
        arrived(k)

    each(p1)
    each(p2, 0)
    for f in flows:
        p1(f, 1).wait_recv()
        wires.go(p1half(f, 1))
        for d in DIRS:
            wires.go(p2(f, 1, d))
    for f in flows:
        p1(f, -1).wait_recv()
        wires.go(p1half(f, -1))
    relay(0)
    each(p2, 3)
    complete(0)
    t0 = flow(0)
    next(t0)
    relay(1)
    for f in flows:
        for d in DIRS:
            p1half(f, d).wait_recv()
    each(p2, 2)
    next(t0)
    complete(1)
    t1 = flow(1)
    next(t1)
    next(t0)
    relay(3)
    next(t0)
    next(t1)
    complete(3)
    t3 = flow(3)
    next(t3)
    next(t1)
    next(t0)
    relay(2)
    next(t1)
    next(t3)
    next(t0)
    complete(2)
    t2 = flow(2)
    next(t2)
    next(t3)
    next(t1)
    next(t2)
    next(t3)
    next(t1)
    next(t2)
    next(t3)
    next(t2)
    next(t3)
    next(t2)
    next(t2)
    for t in (t0, t1, t3, t2):
        for _ in t:
            pass


def by_rows(rows, body):
    def step(i, carry):
        body(pl.ds(pl.multiple_of(i * CHUNK, CHUNK), CHUNK))
        return carry

    lax.fori_loop(0, rows // CHUNK, step, 0)


def tok_flow(wires, tag, k, part, out, r1, s1, r2, r3, s3, epilogue):
    z, core = column()
    other = tok_peer(z, 1 - core)
    me = core * SIDE + z

    def peer(d):
        return tok_peer(ring(z, d), core)

    def swap(j):
        at = ring(z, j)
        return wires.copy((tag, k, 0, j), part.at[k, (1 - core) * SIDE + at], r1.at[k, j], other)

    def far(d):
        return wires.copy((tag, k, 1, d), s1.at[k, 2, rows_of(d)], r2.at[k, s(d)], peer(d))

    def plain(d):
        src = s1.at[k, 1 if d == 1 else 3, rows_of(-d)]
        return wires.copy((tag, k, 2, d), src, r3.at[k, s(d), rows_of(-d)], peer(d))

    def summed(d):
        return wires.copy((tag, k, 3, d), s3.at[k, s(d)], r3.at[k, s(d), rows_of(d)], peer(d))

    def spread(d):
        return wires.copy((tag, k, 4, d), out.at[k, me], out.at[k, me], peer(d))

    def forward(d):
        at = out.at[k, core * SIDE + ring(z, -d), rows_of(d)]
        return wires.copy((tag, k, 5, d), at, at, peer(d))

    def hand(j):
        at = out.at[k, core * SIDE + ring(z, j)]
        return wires.copy((tag, k, 6, j), at, at, other)

    def first(j):
        swap(j).wait_recv()
        at = core * SIDE + ring(z, j)

        def add(i):
            s1[k, j, i] = (f32(part[k, at, i]) + f32(r1[k, j, i])).astype(s1.dtype)

        by_rows(UNIT, add)

    for j in (2, 1, 3, 0):
        wires.go(swap(j))
    yield
    first(2)
    for d in DIRS:
        wires.go(far(d))
    for d in DIRS:
        first(1 if d == 1 else 3)
        wires.go(plain(d))
    first(0)
    yield
    for d in DIRS:
        far(d).wait_recv()
        s3[k, s(d)] = (f32(s1[k, 1 if d == 1 else 3, rows_of(d)]) + f32(r2[k, s(d)])).astype(s3.dtype)
        wires.go(summed(d))
    yield
    for d in DIRS:
        plain(d).wait_recv()
        summed(d).wait_recv()

    def last(i):
        total = f32(s1[k, 0, i]) + f32(r3[k, 0, i]) + f32(r3[k, 1, i])
        out[k, me, i] = epilogue(k, me, i, total).astype(out.dtype)

    by_rows(UNIT, last)
    for d in DIRS:
        wires.go(spread(d))
    wires.go(hand(0))
    yield
    for d in DIRS:
        spread(d).wait_recv()
        wires.go(forward(d))
        wires.go(hand(3 if d == 1 else 1))
    yield
    for d in DIRS:
        forward(d).wait_recv()
    wires.go(hand(2))
    yield
    for j in range(SIDE):
        hand(j).wait_recv()
    yield


def tok_buffers(dtype, width):
    return [
        pltpu.VMEM((SIDE, SIDE, UNIT, width), dtype),
        pltpu.VMEM((SIDE, SIDE, UNIT, width), dtype),
        pltpu.VMEM((SIDE, 2, HALF, width), dtype),
        pltpu.VMEM((SIDE, 2, UNIT, width), dtype),
        pltpu.VMEM((SIDE, 2, HALF, width), dtype),
    ]


def blocks(count, body):
    def step(i, carry):
        body(i)
        return carry

    lax.fori_loop(0, count, step, 0)


def own_tile(k):
    x, y = plane()
    z, core = column()
    return (1 - core) * (z * SIDE + ring(x, -k)) + core * (ring(y, -k) * SIDE + z)


QUAD = 4


def forward_kernel(x, enc, bias, mask, sq, xs, feat, sq_sum, held, part, feats, *rest):
    bufs, (sq_a, sq_b, local, send, recv) = rest[:5], rest[5:]
    wires = Wires(send, recv)
    z, core = column()
    flows = [Flow(h) for h in FLOWS]
    greet()
    slab_count, depth, width = enc.shape
    keep = [pltpu.make_async_copy(x.at[f.h], held.at[0, f.unit(0)], local.at[f.h]) for f in flows]
    for copy in keep:
        copy.start()
    saves = [pltpu.make_async_copy(held.at[k], xs.at[k], local.at[2 + k]) for k in range(SIDE)]
    saves_f = [pltpu.make_async_copy(feats.at[k], feat.at[k], local.at[6 + k]) for k in range(SIDE)]

    def epilogue(k, me, i, total):
        live = mask[own_tile(k)] > 0.0
        return jnp.where(live, jnp.maximum(total + bias[...], 0.0), 0.0)

    def arrived(k):
        if k == 0:
            for copy in keep:
                copy.wait()
        saves[k].start()

        def encode(i):
            slab, quad = lax.div(i, 2), lax.rem(i, 2)
            rows = held[k, pl.ds(quad * QUAD, QUAD)].reshape(QUAD * UNIT, depth)
            at = pl.ds(pl.multiple_of(slab * width, width), width)
            value = jnp.dot(rows, enc[slab], preferred_element_type=F32)
            part[k, pl.ds(quad * QUAD, QUAD), :, at] = value.reshape(QUAD, UNIT, width)

        blocks(2 * slab_count, encode)

    def flow(k):
        yield from tok_flow(wires, "f", k, part, feats, *bufs, epilogue)

    other = tok_peer(z, 1 - core)
    swap = wires.copy("sq", sq, sq_a.at[0], other)
    wires.go(swap)
    swap.wait_recv()
    sq_b[0] = sq[...] + sq_a[0]
    rounds = []
    for d in DIRS:
        rounds.append(wires.copy(("sq", d), sq_b.at[0], sq_b.at[1 + s(d)], tok_peer(ring(z, d), core)))
        wires.go(rounds[-1])
    sweep(wires, "x", lambda h: x.at[h], held, arrived, flow)
    for copy in rounds:
        copy.wait_recv()
    on = wires.copy(("sq", 2), sq_b.at[1], sq_b.at[3], tok_peer(ring(z, 1), core))
    wires.go(on)
    on.wait_recv()
    sq_sum[...] = (sq_b[0] + sq_b[3]) + (sq_b[1] + sq_b[2])
    for copy in saves_f:
        copy.start()
    for copy in saves + saves_f:
        copy.wait()
    wires.drain()


VMEM = pl.BlockSpec(memory_space=pltpu.VMEM)
ANY = pl.BlockSpec(memory_space=pl.ANY)


def forward(x, enc, bias, mask, sq):
    depth = x.shape[2]
    width = bias.shape[1]
    units = (SIDE, 2 * SIDE, UNIT)
    return pl.pallas_call(
        forward_kernel,
        out_shape=[
            jax.ShapeDtypeStruct(units + (depth,), BF16),
            jax.ShapeDtypeStruct(units + (width,), BF16),
            jax.ShapeDtypeStruct(sq.shape, F32),
        ],
        in_specs=[VMEM] * 5,
        out_specs=[ANY, ANY, VMEM],
        scratch_shapes=[
            pltpu.VMEM(units + (depth,), BF16),
            pltpu.VMEM(units + (width,), F32),
            pltpu.VMEM(units + (width,), BF16),
        ]
        + tok_buffers(F32, width)
        + [
            pltpu.VMEM((1,) + sq.shape, F32),
            pltpu.VMEM((4,) + sq.shape, F32),
            pltpu.SemaphoreType.DMA((10,)),
            pltpu.SemaphoreType.DMA((124,)),
            pltpu.SemaphoreType.DMA((124,)),
        ],
        compiler_params=pltpu.CompilerParams(
            vmem_limit_bytes=60 * 1024 * 1024, collective_id=0, has_side_effects=True
        ),
        name="forward",
    )(x, enc, bias, mask, sq)


def backward_kernel(
    scale, x, dec, bias, feats, norm, es, grads, part, r1, r2, s2, c, r4, r5, s5, err, gpart, out, *rest
):
    bufs, (local, send, recv) = rest[:5], rest[5:]
    wires = Wires(send, recv)
    flows = [Flow(h) for h in FLOWS]
    greet()
    width, depth = dec.shape
    cols = 512

    def decode(k):
        def step(i):
            col, quad = lax.div(i, 2), lax.rem(i, 2)
            at = pl.ds(pl.multiple_of(col * cols, cols), cols)
            f = feats[k, pl.ds(quad * QUAD, QUAD)].reshape(QUAD * UNIT, width)
            value = jnp.dot(f, dec[:, at], preferred_element_type=F32)
            part[k, pl.ds(quad * QUAD, QUAD), :, at] = value.reshape(QUAD, UNIT, cols).astype(BF16)

        blocks(2 * (depth // cols), step)

    def far(f, k, d):
        src = part.at[k, f.unit(2), rows_of(d)]
        return wires.copy((0, f.h, k, d), src, r1.at[f.h, k, s(d)], f.near(0, d))

    def plain(f, k, d):
        src = part.at[k, f.unit(d), rows_of(-d)]
        return wires.copy((1, f.h, k, d), src, r2.at[f.h, k, s(d), rows_of(-d)], f.near(0, d))

    def summed(f, k, d):
        src = s2.at[f.h, k, s(d)]
        return wires.copy((2, f.h, k, d), src, r2.at[f.h, k, s(d), rows_of(d)], f.near(0, d))

    def far2(f, d):
        return wires.copy((3, f.h, d), c.at[f.h, 2, rows_of(d)], r4.at[f.h, s(d)], f.near(d, 0))

    def plain2(f, d):
        src = c.at[f.h, 3 if d == 1 else 1, rows_of(-d)]
        return wires.copy((4, f.h, d), src, r5.at[f.h, s(d), rows_of(-d)], f.near(d, 0))

    def summed2(f, d):
        return wires.copy((5, f.h, d), s5.at[f.h, s(d)], r5.at[f.h, s(d), rows_of(d)], f.near(d, 0))

    def add_far(f, k):
        for d in DIRS:
            far(f, k, d).wait_recv()
            s2[f.h, k, s(d)] = (f32(part[k, f.unit(d), rows_of(d)]) + f32(r1[f.h, k, s(d)])).astype(BF16)
            wires.go(summed(f, k, d))

    def reduce(f, k):
        for d in DIRS:
            plain(f, k, d).wait_recv()
            summed(f, k, d).wait_recv()

        def add(i):
            total = f32(part[k, f.unit(0), i]) + f32(r2[f.h, k, 0, i]) + f32(r2[f.h, k, 1, i])
            c[f.h, k, i] = total.astype(BF16)

        by_rows(UNIT, add)

    def begin(k):
        decode(k)
        for f in flows:
            for d in DIRS:
                wires.go(far(f, k, d))
        for f in flows:
            for d in DIRS:
                wires.go(plain(f, k, d))

    def relay(k):
        for f in flows:
            add_far(f, k)

    begin(2)
    begin(1)
    relay(2)
    begin(3)
    relay(1)
    begin(0)
    for f in flows:
        reduce(f, 2)
        for d in DIRS:
            wires.go(far2(f, d))
    relay(3)
    for f in flows:
        reduce(f, 1)
        wires.go(plain2(f, -1))
    relay(0)
    for f in flows:
        reduce(f, 3)
        wires.go(plain2(f, 1))
    for f in flows:
        for d in DIRS:
            far2(f, d).wait_recv()
            s5[f.h, s(d)] = (f32(c[f.h, 3 if d == 1 else 1, rows_of(d)]) + f32(r4[f.h, s(d)])).astype(BF16)
            wires.go(summed2(f, d))
    for f in flows:
        reduce(f, 0)
    for f in flows:
        for d in DIRS:
            plain2(f, d).wait_recv()
            summed2(f, d).wait_recv()

        def finish(i):
            recon = f32(c[f.h, 0, i]) + f32(r5[f.h, 0, i]) + f32(r5[f.h, 1, i]) + bias[...]
            err[0, f.unit(0), i] = (recon - f32(x[f.h, i])).astype(BF16)

        by_rows(UNIT, finish)

    saves = [pltpu.make_async_copy(err.at[k], es.at[k], local.at[k]) for k in range(SIDE)]
    saves_g = [pltpu.make_async_copy(out.at[k], grads.at[k], local.at[4 + k]) for k in range(SIDE)]

    def arrived(k):
        saves[k].start()

        def step(i):
            slab, quad = lax.div(i, 2), lax.rem(i, 2)
            at = pl.ds(pl.multiple_of(slab * 256, 256), 256)
            e = err[k, pl.ds(quad * QUAD, QUAD)].reshape(QUAD * UNIT, depth)
            value = lax.dot_general(e, dec[at], NT, preferred_element_type=F32)
            gpart[k, pl.ds(quad * QUAD, QUAD), :, at] = value.reshape(QUAD, UNIT, 256).astype(BF16)

        blocks(2 * (width // 256), step)

    def epilogue(k, me, i, total):
        grad = scale * (total + SPARSITY * norm[...])
        return jnp.where(f32(feats[k, me, i]) > 0.0, grad, 0.0)

    def flow(k):
        yield from tok_flow(wires, "g", k, gpart, out, *bufs, epilogue)

    sweep(wires, "e", lambda h: err.at[0, flows[h].unit(0)], err, arrived, flow)
    for copy in saves_g:
        copy.start()
    for copy in saves + saves_g:
        copy.wait()
    wires.drain()


def backward(scale, x, dec, bias, feats, norm):
    width, depth = dec.shape
    units = (SIDE, 2 * SIDE, UNIT)
    return pl.pallas_call(
        functools.partial(backward_kernel, scale),
        out_shape=[
            jax.ShapeDtypeStruct(units + (depth,), BF16),
            jax.ShapeDtypeStruct(units + (width,), BF16),
        ],
        in_specs=[VMEM] * 5,
        out_specs=[ANY, ANY],
        scratch_shapes=[
            pltpu.VMEM(units + (depth,), BF16),
            pltpu.VMEM((2, SIDE, 2, HALF, depth), BF16),
            pltpu.VMEM((2, SIDE, 2, UNIT, depth), BF16),
            pltpu.VMEM((2, SIDE, 2, HALF, depth), BF16),
            pltpu.VMEM((2, SIDE, UNIT, depth), BF16),
            pltpu.VMEM((2, 2, HALF, depth), BF16),
            pltpu.VMEM((2, 2, UNIT, depth), BF16),
            pltpu.VMEM((2, 2, HALF, depth), BF16),
            pltpu.VMEM(units + (depth,), BF16),
            pltpu.VMEM(units + (width,), BF16),
            pltpu.VMEM(units + (width,), BF16),
        ]
        + tok_buffers(BF16, width)
        + [
            pltpu.SemaphoreType.DMA((8,)),
            pltpu.SemaphoreType.DMA((190,)),
            pltpu.SemaphoreType.DMA((190,)),
        ],
        compiler_params=pltpu.CompilerParams(
            vmem_limit_bytes=60 * 1024 * 1024, collective_id=1, has_side_effects=True
        ),
        name="backward",
    )(x, dec, bias, feats, norm)


def on_device(activations, enc_weight, enc_bias, dec_weight, dec_bias, active):
    slabs, models, depth, block = enc_weight.shape
    rows = activations.shape[0]
    width = slabs * block
    scale = 1.0 / math.sqrt(MOST * TILE)
    first = lax.axis_index("lat") * slabs
    ids = first + jnp.arange(slabs, dtype=jnp.int32)
    live = jnp.any(active[:, :, None] == ids[None, None, :], axis=1).astype(F32)
    mask = jnp.broadcast_to(live[:, None, :, None], (active.shape[0], 1, slabs, block))
    mask = mask.reshape(active.shape[0], 1, width)
    x = activations.reshape(2, rows // 2, models * depth)
    dec = dec_weight.reshape(width, models * depth)
    dec_wide = dec.reshape(width, models, depth).astype(F32)
    sq = jnp.sum(jnp.square(dec_wide), axis=2).T
    enc = enc_weight.reshape(slabs, models * depth, block)
    xs, feats, sq_sum = forward(x, enc, enc_bias.reshape(1, width), mask, sq)
    norms = jnp.sqrt(sq_sum + NORM_EPSILON)
    es, grads = backward(
        scale,
        x,
        dec,
        dec_bias.reshape(1, models * depth),
        feats,
        jnp.sum(norms, axis=0, keepdims=True),
    )
    count = active.shape[0] * rows
    xs, es = xs.reshape(count, models, depth), es.reshape(count, models, depth)
    feats, grads = feats.reshape(count, width), grads.reshape(count, slabs, block)
    grad_enc = jnp.einsum("rmd,rsj->smdj", xs, grads, preferred_element_type=F32).astype(BF16)
    grad_enc_bias = jnp.sum(grads.astype(F32), axis=0)
    feat_total = jnp.sum(feats.astype(F32), axis=0)
    recon_term = jnp.einsum("rj,rmd->jmd", feats, es, preferred_element_type=F32)
    norm_term = (SPARSITY * feat_total[:, None] / norms.T)[:, :, None] * dec_wide
    grad_dec = (scale * (recon_term + norm_term)).astype(BF16)
    grad_dec_bias = scale * jnp.sum(es.astype(F32), axis=0)
    return (grad_enc, grad_enc_bias, grad_dec.reshape(dec_weight.shape), grad_dec_bias)


def solution(mesh):
    placed = (
        P("lat", None, "tok"),
        P("lat", None, "tok", None),
        P("lat", None),
        P("lat", None, None, "tok"),
        P(None, "tok"),
        P(),
    )
    return jax.shard_map(
        on_device,
        mesh=mesh,
        in_specs=placed,
        out_specs=(
            P("lat", None, "tok", None),
            P("lat", None),
            P("lat", None, None, "tok"),
            P(None, "tok"),
        ),
        check_vma=False,
    )
```

```python
import functools
import math

import jax
import jax.numpy as jnp
from jax import lax
from jax.experimental import pallas as pl
from jax.experimental.pallas import tpu as pltpu
from jax.sharding import PartitionSpec as P

MOST = 8
TILE = 128
SPARSITY = 0.25
NORM_EPSILON = 1e-06
MESH = pl.DeviceIdType.MESH
SIDE = 4
UNIT = TILE // 2
HALF = UNIT // 2
CHUNK = 32
DIRS = (1, -1)
ORDER = (0, 1, 3, 2)
BF16, F32 = jnp.bfloat16, jnp.float32
NT = (((1,), (1,)), ((), ()))
TN = (((0,), (0,)), ((), ()))


def ring(i, step):
    return lax.rem(i + step + SIDE, SIDE)


def lat_peer(y, x):
    return {"lat": y * SIDE + x}


def tok_peer(z, core):
    return {"tok": z * 2 + core}


def plane():
    lat = lax.axis_index("lat")
    return lax.rem(lat, SIDE), lax.div(lat, SIDE)


def column():
    tok = lax.axis_index("tok")
    return lax.div(tok, 2), lax.rem(tok, 2)


def greet():
    x, y = plane()
    z, core = column()
    peers = [lat_peer(y, ring(x, d)) for d in DIRS] + [lat_peer(ring(y, d), x) for d in DIRS]
    peers += [tok_peer(ring(z, d), core) for d in DIRS] + [tok_peer(z, 1 - core)]
    barrier = pltpu.get_barrier_semaphore()
    for peer in peers:
        pl.semaphore_signal(barrier, inc=1, device_id=peer, device_id_type=MESH)
    pl.semaphore_wait(barrier, len(peers))


def s(d):
    return 0 if d == 1 else 1


def rows_of(d):
    return pl.ds(0 if d == 1 else HALF, HALF)


def f32(v):
    return v.astype(F32)


class Wires:
    def __init__(self, send, recv):
        self.send, self.recv = send, recv
        self.numbers, self.started = {}, []

    def copy(self, key, src, dst, peer):
        n = self.numbers.setdefault(key, len(self.numbers))
        return pltpu.make_async_remote_copy(
            src_ref=src,
            dst_ref=dst,
            send_sem=self.send.at[n],
            recv_sem=self.recv.at[n],
            device_id=peer,
            device_id_type=MESH,
        )

    def go(self, copy, source=None):
        copy.start()
        self.started.append((source, copy))

    def settle(self, source):
        for name, copy in self.started:
            if name == source:
                copy.wait_send()
        self.started = [item for item in self.started if item[0] != source]

    def drain(self):
        for _, copy in self.started:
            copy.wait_send()


FLOWS = (0, 1)


class Flow:
    def __init__(self, h):
        x, y = plane()
        self.h = h
        self.p, self.q = (x, y) if h == 0 else (y, x)

    def near(self, dp, dq):
        p, q = ring(self.p, dp), ring(self.q, dq)
        return lat_peer(q, p) if self.h == 0 else lat_peer(p, q)

    def unit(self, dq):
        return self.h * SIDE + ring(self.q, dq)


class Gather:
    def __init__(self, wires, flows, tag, own, held, own_source):
        self.wires, self.flows, self.tag = wires, flows, tag
        self.own, self.held, self.own_source = own, held, own_source

    def p1(self, f, d):
        dst = self.held.at[1 if d == 1 else 3, f.unit(0)]
        return self.wires.copy((self.tag, 0, f.h, d), self.own(f.h), dst, f.near(d, 0))

    def p1half(self, f, d):
        src = self.held.at[1 if d == 1 else 3, f.unit(0), rows_of(d)]
        dst = self.held.at[2, f.unit(0), rows_of(d)]
        return self.wires.copy((self.tag, 1, f.h, d), src, dst, f.near(d, 0))

    def p2(self, f, k, d):
        at = self.held.at[k, f.unit(0)]
        return self.wires.copy((self.tag, 2, f.h, k, d), self.own(f.h) if k == 0 else at, at, f.near(0, d))

    def p2half(self, f, k, d):
        at = self.held.at[k, f.unit(-d), rows_of(d)]
        return self.wires.copy((self.tag, 3, f.h, k, d), at, at, f.near(0, d))

    def name(self, k):
        return (self.tag, k)

    def send(self, k):
        for f in self.flows:
            for d in DIRS:
                self.wires.go(self.p2(f, k, d), self.own_source if k == 0 else self.name(k))

    def begin(self):
        for f in self.flows:
            for d in DIRS:
                self.wires.go(self.p1(f, d), self.own_source)
        self.send(0)
        for d, k in ((1, 1), (-1, 3)):
            for f in self.flows:
                self.p1(f, d).wait_recv()
                self.wires.go(self.p1half(f, d), self.name(k))
            self.send(k)

    def far(self):
        for f in self.flows:
            for d in DIRS:
                self.p1half(f, d).wait_recv()
        self.send(2)

    def relay(self, k):
        for f in self.flows:
            for d in DIRS:
                self.p2(f, k, d).wait_recv()
                self.wires.go(self.p2half(f, k, d), self.name(k))

    def complete(self, k):
        for f in self.flows:
            for d in DIRS:
                self.p2half(f, k, d).wait_recv()


def by_rows(rows, body):
    def step(i, carry):
        body(pl.ds(pl.multiple_of(i * CHUNK, CHUNK), CHUNK))
        return carry

    lax.fori_loop(0, rows // CHUNK, step, 0)


def tok_flow(wires, tag, k, part, out, r1, s1, r2, r3, epilogue):
    n = ORDER.index(k) % 2
    z, core = column()
    other = tok_peer(z, 1 - core)
    me = core * SIDE + z
    inputs, sums = (tag, k, "in"), (tag, k, "sum")

    def peer(d):
        return tok_peer(ring(z, d), core)

    def swap(j):
        at = ring(z, j)
        return wires.copy((tag, k, 0, j), part.at[n, (1 - core) * SIDE + at], r1.at[n, j], other)

    def far(d):
        return wires.copy((tag, k, 1, d), s1.at[n, 2, rows_of(d)], r2.at[n, s(d)], peer(d))

    def plain(d):
        src = s1.at[n, 1 if d == 1 else 3, rows_of(-d)]
        return wires.copy((tag, k, 2, d), src, r3.at[n, s(d), rows_of(-d)], peer(d))

    def summed(d):
        src = s1.at[n, 1 if d == 1 else 3, rows_of(d)]
        return wires.copy((tag, k, 3, d), src, r3.at[n, s(d), rows_of(d)], peer(d))

    def spread(d):
        return wires.copy((tag, k, 4, d), out.at[k, me], out.at[k, me], peer(d))

    def forward(d):
        at = out.at[k, core * SIDE + ring(z, -d), rows_of(d)]
        return wires.copy((tag, k, 5, d), at, at, peer(d))

    def hand(j):
        at = out.at[k, core * SIDE + ring(z, j)]
        return wires.copy((tag, k, 6, j), at, at, other)

    def first(j):
        swap(j).wait_recv()
        at = core * SIDE + ring(z, j)

        def add(i):
            s1[n, j, i] = (f32(part[n, at, i]) + f32(r1[n, j, i])).astype(s1.dtype)

        by_rows(UNIT, add)

    for j in (2, 1, 3, 0):
        wires.go(swap(j), inputs)
    yield
    first(2)
    for d in DIRS:
        wires.go(far(d), sums)
    for d in DIRS:
        first(1 if d == 1 else 3)
        wires.go(plain(d), sums)
    first(0)
    yield
    for d in DIRS:
        far(d).wait_recv()
        j = 1 if d == 1 else 3
        s1[n, j, rows_of(d)] = (f32(s1[n, j, rows_of(d)]) + f32(r2[n, s(d)])).astype(s1.dtype)
        wires.go(summed(d), sums)
    yield
    for d in DIRS:
        plain(d).wait_recv()
        summed(d).wait_recv()

    def last(i):
        total = f32(s1[n, 0, i]) + f32(r3[n, 0, i]) + f32(r3[n, 1, i])
        out[k, me, i] = epilogue(k, me, i, total).astype(out.dtype)

    by_rows(UNIT, last)
    for d in DIRS:
        wires.go(spread(d))
    wires.go(hand(0))
    yield
    for d in DIRS:
        spread(d).wait_recv()
        wires.go(forward(d))
        wires.go(hand(3 if d == 1 else 1))
    yield
    for d in DIRS:
        forward(d).wait_recv()
    wires.go(hand(2))
    yield
    for j in range(SIDE):
        hand(j).wait_recv()
    wires.settle(inputs)
    wires.settle(sums)
    yield


def tok_buffers(dtype, width):
    return [
        pltpu.VMEM((2, 2 * SIDE, UNIT, width), dtype),
        pltpu.VMEM((2, SIDE, UNIT, width), dtype),
        pltpu.VMEM((2, SIDE, UNIT, width), dtype),
        pltpu.VMEM((2, 2, HALF, width), dtype),
        pltpu.VMEM((2, 2, UNIT, width), dtype),
    ]


def blocks(count, body):
    def step(i, carry):
        body(i)
        return carry

    lax.fori_loop(0, count, step, 0)


def own_tile(k):
    x, y = plane()
    z, core = column()
    return (1 - core) * (z * SIDE + ring(x, -k)) + core * (ring(y, -k) * SIDE + z)


QUAD = 4


def step_kernel(
    scale,
    x,
    enc,
    dec,
    enc_bias,
    dec_bias,
    mask,
    sq,
    xs,
    es,
    feat_out,
    grad_out,
    sq_sum,
    held,
    err,
    feats,
    grads,
    r1,
    r2,
    r4,
    r5,
    norm,
    sq_a,
    sq_b,
    *rest,
):
    fwd, bwd, (local, send, recv) = rest[:5], rest[5:10], rest[10:]
    wires = Wires(send, recv)
    z, core = column()
    flows = [Flow(h) for h in FLOWS]
    slab_count, depth, block = enc.shape
    width = dec.shape[0]
    cols = 512
    keep = [pltpu.make_async_copy(x.at[f.h], held.at[0, f.unit(0)], local.at[f.h]) for f in flows]
    saves = {}

    def save(name, k, src, dst):
        n = 2 + len(saves)
        saves[name, k] = pltpu.make_async_copy(src.at[k], dst.at[k], local.at[n])
        saves[name, k].start()

    for copy in keep:
        copy.start()
    greet()


    def feature(k, me, i, total):
        live = mask[own_tile(k)] > 0.0
        return jnp.where(live, jnp.maximum(total + enc_bias[...], 0.0), 0.0)

    def encode(k):
        n = ORDER.index(k) % 2

        def step(i):
            slab, quad = lax.div(i, 2), lax.rem(i, 2)
            rows = held[k, pl.ds(quad * QUAD, QUAD)].reshape(QUAD * UNIT, depth)
            at = pl.ds(pl.multiple_of(slab * block, block), block)
            value = jnp.dot(rows, enc[slab], preferred_element_type=F32)
            fwd[0][n, pl.ds(quad * QUAD, QUAD), :, at] = value.reshape(QUAD, UNIT, block)

        blocks(2 * slab_count, step)

    swap = wires.copy("sq", sq, sq_a.at[0], tok_peer(z, 1 - core))
    turns = [wires.copy(("sq", d), sq_b.at[0], sq_b.at[1 + s(d)], tok_peer(ring(z, d), core)) for d in DIRS]
    turn_on = wires.copy(("sq", 2), sq_b.at[1], sq_b.at[3], tok_peer(ring(z, 1), core))

    def gather_steps(g, tag, bufs, out, work, epilogue, save_rows, save_out, between):
        t = {k: tok_flow(wires, tag, k, bufs[0], out, *bufs[1:], epilogue) for k in ORDER}

        def arrive(k):
            g.complete(k)
            save_rows(k)
            work(k)
            next(t[k])

        def go(k, count=1):
            for _ in range(count):
                next(t[k])

        def end(k):
            go(k)
            save_out(k)

        g.begin()
        g.relay(0)
        g.far()
        arrive(0)
        between(0)
        go(0)
        g.relay(1)
        go(0)
        arrive(1)
        between(1)
        go(0, 2)
        go(1)
        g.relay(3)
        go(1)
        go(0)
        end(0)
        arrive(3)
        between(2)
        go(1, 2)
        go(3)
        g.relay(2)
        go(3)
        go(1)
        end(1)
        arrive(2)
        yield
        go(3, 2)
        go(2)
        yield
        go(2)
        go(3)
        end(3)
        yield
        go(2, 2)
        yield
        go(2)
        end(2)
        yield

    def own_x(h):
        return x.at[h]

    def norms(stage):
        if stage == 0:
            swap.wait_recv()
            sq_b[0] = sq[...] + sq_a[0]
            for copy in turns:
                wires.go(copy)
        elif stage == 1:
            for copy in turns:
                copy.wait_recv()
            wires.go(turn_on)
        else:
            turn_on.wait_recv()
            total = (sq_b[0] + sq_b[3]) + (sq_b[1] + sq_b[2])
            sq_sum[...] = total
            norm[...] = jnp.sum(jnp.sqrt(total + NORM_EPSILON), axis=0, keepdims=True)

    wires.go(swap)
    front = Gather(wires, flows, "x", own_x, held, "own x")

    def save_x(k):
        if k == 0:
            for copy in keep:
                copy.wait()
        save("x", k, held, xs)

    steps = gather_steps(
        front, "f", fwd, feats, encode, feature, save_x, lambda k: save("f", k, feats, feat_out), norms
    )
    next(steps)


    def decode(k):
        wires.settle(front.name(k))
        saves["x", k].wait()

        def step(i):
            col, quad = lax.div(i, 2), lax.rem(i, 2)
            at = pl.ds(pl.multiple_of(col * cols, cols), cols)
            f = feats[k, pl.ds(quad * QUAD, QUAD)].reshape(QUAD * UNIT, width)
            value = jnp.dot(f, dec[:, at], preferred_element_type=F32)
            held[k, pl.ds(quad * QUAD, QUAD), :, at] = value.reshape(QUAD, UNIT, cols).astype(BF16)

        blocks(2 * (depth // cols), step)

    def far(f, k, d):
        src = held.at[k, f.unit(2), rows_of(d)]
        return wires.copy((0, f.h, k, d), src, r1.at[f.h, k, s(d)], f.near(0, d))

    def plain(f, k, d):
        src = held.at[k, f.unit(d), rows_of(-d)]
        return wires.copy((1, f.h, k, d), src, r2.at[f.h, k, s(d), rows_of(-d)], f.near(0, d))

    def summed(f, k, d):
        src = held.at[k, f.unit(d), rows_of(d)]
        return wires.copy((2, f.h, k, d), src, r2.at[f.h, k, s(d), rows_of(d)], f.near(0, d))

    def far2(f, d):
        src = held.at[2, f.unit(0), rows_of(d)]
        return wires.copy((3, f.h, d), src, r4.at[f.h, s(d)], f.near(d, 0))

    def plain2(f, d):
        src = held.at[3 if d == 1 else 1, f.unit(0), rows_of(-d)]
        return wires.copy((4, f.h, d), src, r5.at[f.h, s(d), rows_of(-d)], f.near(d, 0))

    def summed2(f, d):
        src = held.at[3 if d == 1 else 1, f.unit(0), rows_of(d)]
        return wires.copy((5, f.h, d), src, r5.at[f.h, s(d), rows_of(d)], f.near(d, 0))

    def begin(k):
        decode(k)
        for f in flows:
            for d in DIRS:
                wires.go(far(f, k, d))
        for f in flows:
            for d in DIRS:
                wires.go(plain(f, k, d))

    def relay(k):
        for f in flows:
            for d in DIRS:
                far(f, k, d).wait_recv()
                at = (k, f.unit(d), rows_of(d))
                held[at] = (f32(held[at]) + f32(r1[f.h, k, s(d)])).astype(BF16)
                wires.go(summed(f, k, d))

    def reduce(k):
        for f in flows:
            for d in DIRS:
                plain(f, k, d).wait_recv()
                summed(f, k, d).wait_recv()

            def add(i, f=f):
                total = f32(held[k, f.unit(0), i]) + f32(r2[f.h, k, 0, i]) + f32(r2[f.h, k, 1, i])
                held[k, f.unit(0), i] = total.astype(BF16)

            by_rows(UNIT, add)

    begin(0)
    next(steps)
    begin(1)
    relay(0)
    next(steps)
    begin(3)
    next(steps)
    relay(1)
    reduce(0)
    next(steps)
    begin(2)
    relay(3)
    reduce(1)
    for f in flows:
        wires.go(plain2(f, -1))
    relay(2)
    reduce(3)
    for f in flows:
        wires.go(plain2(f, 1))
    reduce(2)
    for f in flows:
        for d in DIRS:
            wires.go(far2(f, d))
    for f in flows:
        for d in DIRS:
            far2(f, d).wait_recv()
            at = (3 if d == 1 else 1, f.unit(0), rows_of(d))
            held[at] = (f32(held[at]) + f32(r4[f.h, s(d)])).astype(BF16)
            wires.go(summed2(f, d))
    for f in flows:
        for d in DIRS:
            plain2(f, d).wait_recv()
            summed2(f, d).wait_recv()

        def finish(i, f=f):
            recon = f32(held[0, f.unit(0), i]) + f32(r5[f.h, 0, i]) + f32(r5[f.h, 1, i]) + dec_bias[...]
            err[0, f.unit(0), i] = (recon - f32(x[f.h, i])).astype(BF16)

        by_rows(UNIT, finish)


    def project(k):
        n = ORDER.index(k) % 2

        def step(i):
            slab, quad = lax.div(i, 2), lax.rem(i, 2)
            at = pl.ds(pl.multiple_of(slab * block, block), block)
            e = err[k, pl.ds(quad * QUAD, QUAD)].reshape(QUAD * UNIT, depth)
            value = lax.dot_general(e, dec[at], NT, preferred_element_type=F32)
            bwd[0][n, pl.ds(quad * QUAD, QUAD), :, at] = value.reshape(QUAD, UNIT, block).astype(BF16)

        blocks(2 * slab_count, step)

    def pre_grad(k, me, i, total):
        grad = scale * (total + SPARSITY * norm[...])
        return jnp.where(f32(feats[k, me, i]) > 0.0, grad, 0.0)

    back = Gather(wires, flows, "e", lambda h: err.at[0, flows[h].unit(0)], err, "own e")
    for _ in gather_steps(
        back,
        "g",
        bwd,
        grads,
        project,
        pre_grad,
        lambda k: save("e", k, err, es),
        lambda k: save("g", k, grads, grad_out),
        lambda stage: None,
    ):
        pass
    for (name, _), copy in saves.items():
        if name != "x":
            copy.wait()
    wires.drain()


VMEM = pl.BlockSpec(memory_space=pltpu.VMEM)
ANY = pl.BlockSpec(memory_space=pl.ANY)


def step(scale, x, enc, dec, enc_bias, dec_bias, mask, sq):
    width, depth = dec.shape
    units = (SIDE, 2 * SIDE, UNIT)
    rows = jax.ShapeDtypeStruct(units + (depth,), BF16)
    latents = jax.ShapeDtypeStruct(units + (width,), BF16)
    return pl.pallas_call(
        functools.partial(step_kernel, scale),
        out_shape=[rows, rows, latents, latents, jax.ShapeDtypeStruct(sq.shape, F32)],
        in_specs=[VMEM] * 7,
        out_specs=[ANY, ANY, ANY, ANY, VMEM],
        scratch_shapes=[
            pltpu.VMEM(units + (depth,), BF16),
            pltpu.VMEM(units + (depth,), BF16),
            pltpu.VMEM(units + (width,), BF16),
            pltpu.VMEM(units + (width,), BF16),
            pltpu.VMEM((2, SIDE, 2, HALF, depth), BF16),
            pltpu.VMEM((2, SIDE, 2, UNIT, depth), BF16),
            pltpu.VMEM((2, 2, HALF, depth), BF16),
            pltpu.VMEM((2, 2, UNIT, depth), BF16),
            pltpu.VMEM((1, width), F32),
            pltpu.VMEM((1,) + sq.shape, F32),
            pltpu.VMEM((4,) + sq.shape, F32),
        ]
        + tok_buffers(F32, width)
        + tok_buffers(BF16, width)
        + [
            pltpu.SemaphoreType.DMA((18,)),
            pltpu.SemaphoreType.DMA((288,)),
            pltpu.SemaphoreType.DMA((288,)),
        ],
        compiler_params=pltpu.CompilerParams(
            vmem_limit_bytes=60 * 1024 * 1024, collective_id=0, has_side_effects=True
        ),
        name="step",
    )(x, enc, dec, enc_bias, dec_bias, mask, sq)


def weights_kernel(scale, units, count, xs, es, feats, grads, dec, inv_norm, grad_enc, grad_dec, acc_e, acc_d, tot):
    slabs, block = grad_enc.shape[0], grad_enc.shape[2]
    for slab in range(slabs):
        at = pl.ds(slab * block, block)
        acc_e[...] = jnp.zeros_like(acc_e)
        acc_d[...] = jnp.zeros_like(acc_d)
        tot[...] = jnp.zeros_like(tot)

        def pair(i, carry, slab=slab, at=at):
            ids = [units[slab * 2 * MOST + i * QUAD + n] for n in range(QUAD)]
            f = jnp.concatenate([feats[n, :, at] for n in ids], axis=0)
            g = jnp.concatenate([grads[n, :, at] for n in ids], axis=0)
            a = jnp.concatenate([xs[n] for n in ids], axis=0)
            e = jnp.concatenate([es[n] for n in ids], axis=0)
            acc_e[...] += lax.dot_general(a, g, TN, preferred_element_type=F32)
            acc_d[...] += lax.dot_general(f, e, TN, preferred_element_type=F32)
            ones = jnp.ones((QUAD * UNIT, 128), BF16)
            tot[...] += lax.dot_general(f, ones, TN, preferred_element_type=F32)
            return carry

        lax.fori_loop(0, lax.div(count[slab] + 1, 2), pair, 0)
        grad_enc[slab] = acc_e[...].astype(grad_enc.dtype)
        col = SPARSITY * tot[:, :1] * inv_norm[at, :]
        grad_dec[at] = (scale * (acc_d[...] + col * f32(dec[at]))).astype(grad_dec.dtype)


def weights(scale, units, count, xs, es, feats, grads, dec, inv_norm, models, slabs):
    width, depth = dec.shape
    cols = 512
    block = width // slabs
    per = depth // models // cols

    def whole(a):
        return pl.BlockSpec(a.shape, lambda c, *_: (0,) * a.ndim)

    def wide(rank):
        return lambda c, *_: (0,) * (rank - 1) + (c,)

    return pl.pallas_call(
        functools.partial(weights_kernel, scale),
        out_shape=[
            jax.ShapeDtypeStruct((slabs, depth, block), BF16),
            jax.ShapeDtypeStruct((width, depth), BF16),
        ],
        grid_spec=pltpu.PrefetchScalarGridSpec(
            num_scalar_prefetch=2,
            grid=(depth // cols,),
            in_specs=[
                pl.BlockSpec(xs.shape[:2] + (cols,), wide(3)),
                pl.BlockSpec(es.shape[:2] + (cols,), wide(3)),
                whole(feats),
                whole(grads),
                pl.BlockSpec((width, cols), wide(2)),
                pl.BlockSpec((None, width, 1), lambda c, *_: (lax.div(c, per), 0, 0)),
            ],
            out_specs=[
                pl.BlockSpec((slabs, cols, block), lambda c, *_: (0, c, 0)),
                pl.BlockSpec((width, cols), wide(2)),
            ],
            scratch_shapes=[
                pltpu.VMEM((cols, block), F32),
                pltpu.VMEM((block, cols), F32),
                pltpu.VMEM((block, 128), F32),
            ],
        ),
        compiler_params=pltpu.CompilerParams(vmem_limit_bytes=56 * 1024 * 1024),
        name="weights",
    )(units, count, xs, es, feats, grads, dec, inv_norm)


def unit_lists(is_active):
    tiles = is_active.shape[0]
    ids = jnp.arange(tiles, dtype=jnp.int32)
    before = (ids[:, None] > ids[None, :]).astype(jnp.int32)
    rank = jnp.sum(before[:, :, None] * is_active[None], axis=1)
    places = jnp.arange(MOST, dtype=jnp.int32)
    picked = (is_active[:, :, None] == 1) & (rank[:, :, None] == places)
    idle = jnp.min(jnp.where(is_active == 0, ids[:, None], tiles - 1), axis=0)
    count = jnp.sum(is_active, axis=0)
    tile = jnp.sum(jnp.where(picked, ids[:, None, None], 0), axis=0)
    tile = jnp.where(places[None, :] < count[:, None], tile, idle[:, None])
    x, y = plane()
    tx, ty = tile % SIDE, tile // SIDE
    one = ((x - tx) % SIDE) * 2 * SIDE + ty
    two = ((y - ty) % SIDE) * 2 * SIDE + SIDE + tx
    return jnp.stack([one, two], axis=2).reshape(-1), count


def on_device(activations, enc_weight, enc_bias, dec_weight, dec_bias, active):
    slabs, models, depth, block = enc_weight.shape
    rows, tiles = activations.shape[0], active.shape[0]
    width = slabs * block
    scale = 1.0 / math.sqrt(MOST * TILE)
    ids = lax.axis_index("lat") * slabs + jnp.arange(slabs, dtype=jnp.int32)
    is_active = jnp.any(active[:, :, None] == ids[None, None, :], axis=1).astype(jnp.int32)
    mask = jnp.broadcast_to(is_active.astype(F32)[:, None, :, None], (tiles, 1, slabs, block))
    mask = mask.reshape(tiles, 1, width)
    units, count = unit_lists(is_active)
    x = activations.reshape(2, rows // 2, models * depth)
    dec = dec_weight.reshape(width, models * depth)
    sq = jnp.stack(
        [jnp.sum(jnp.square(dec[:, m * depth : (m + 1) * depth].astype(F32)), axis=1) for m in range(models)]
    )
    enc = enc_weight.reshape(slabs, models * depth, block)
    xs, es, feats, grads, sq_sum = step(
        scale, x, enc, dec, enc_bias.reshape(1, width), dec_bias.reshape(1, models * depth), mask, sq
    )
    inv_norm = (1.0 / jnp.sqrt(sq_sum + NORM_EPSILON))[:, :, None]
    flat = (2 * tiles, UNIT)
    grad_enc, grad_dec = weights(
        scale,
        units,
        count,
        xs.reshape(flat + (models * depth,)),
        es.reshape(flat + (models * depth,)),
        feats.reshape(flat + (width,)),
        grads.reshape(flat + (width,)),
        dec,
        inv_norm,
        models,
        slabs,
    )
    grad_enc_bias = jnp.sum(grads.astype(F32), axis=(0, 1, 2))
    grad_dec_bias = scale * jnp.sum(es.astype(F32), axis=(0, 1, 2))
    return (
        grad_enc.reshape(enc_weight.shape),
        grad_enc_bias.reshape(slabs, block),
        grad_dec.reshape(dec_weight.shape),
        grad_dec_bias.reshape(models, depth),
    )


def solution(mesh):
    placed = (
        P("lat", None, "tok"),
        P("lat", None, "tok", None),
        P("lat", None),
        P("lat", None, None, "tok"),
        P(None, "tok"),
        P(),
    )
    return jax.shard_map(
        on_device,
        mesh=mesh,
        in_specs=placed,
        out_specs=(
            P("lat", None, "tok", None),
            P("lat", None),
            P("lat", None, None, "tok"),
            P(None, "tok"),
        ),
        check_vma=False,
    )
```

```python
import functools
import math

import jax
import jax.numpy as jnp
from jax import lax
from jax.experimental import pallas as pl
from jax.experimental.pallas import tpu as pltpu
from jax.sharding import PartitionSpec as P

MOST = 8
TILE = 128
SPARSITY = 0.25
NORM_EPSILON = 1e-06
MESH = pl.DeviceIdType.MESH
SIDE = 4
UNIT = TILE // 2
PIECE = UNIT // 2
HALF = PIECE // 2
PIECES = (0, 1)
SLOTS = 4
DIRS = (1, -1)
ORDER = tuple((k, e) for k in (0, 1, 3, 2) for e in PIECES)
BF16, F32 = jnp.bfloat16, jnp.float32
NT = (((1,), (1,)), ((), ()))
TN = (((0,), (0,)), ((), ()))


def ring(i, step):
    return lax.rem(i + step + SIDE, SIDE)


def lat_peer(y, x):
    return {"lat": y * SIDE + x}


def tok_peer(z, core):
    return {"tok": z * 2 + core}


def plane():
    lat = lax.axis_index("lat")
    return lax.rem(lat, SIDE), lax.div(lat, SIDE)


def column():
    tok = lax.axis_index("tok")
    return lax.div(tok, 2), lax.rem(tok, 2)


def greet():
    x, y = plane()
    z, core = column()
    peers = [lat_peer(y, ring(x, d)) for d in DIRS] + [lat_peer(ring(y, d), x) for d in DIRS]
    peers += [tok_peer(ring(z, d), core) for d in DIRS] + [tok_peer(z, 1 - core)]
    barrier = pltpu.get_barrier_semaphore()
    for peer in peers:
        pl.semaphore_signal(barrier, inc=1, device_id=peer, device_id_type=MESH)
    pl.semaphore_wait(barrier, len(peers))


def s(d):
    return 0 if d == 1 else 1


def rows_of(d, e=0):
    return pl.ds(e * PIECE + (0 if d == 1 else HALF), HALF)


def piece(e):
    return pl.ds(e * PIECE, PIECE)


def f32(v):
    return v.astype(F32)


class Wires:
    def __init__(self, send, recv):
        self.send, self.recv = send, recv
        self.numbers, self.started = {}, []

    def copy(self, key, src, dst, peer):
        n = self.numbers.setdefault(key, len(self.numbers))
        return pltpu.make_async_remote_copy(
            src_ref=src,
            dst_ref=dst,
            send_sem=self.send.at[n],
            recv_sem=self.recv.at[n],
            device_id=peer,
            device_id_type=MESH,
        )

    def go(self, copy, source=None):
        copy.start()
        self.started.append((source, copy))

    def settle(self, source):
        for name, copy in self.started:
            if name == source:
                copy.wait_send()
        self.started = [item for item in self.started if item[0] != source]

    def drain(self):
        for _, copy in self.started:
            copy.wait_send()
        self.started = []


FLOWS = (0, 1)
FWD, MID, BWD = range(3)
SEND, CROSS, NEAR, FAR, RELAY, WORK, TOK, NORM, BEGIN, REDUCE, JOIN, FINISH = range(12)
SCRIPT = (
    (FWD, SEND, 0, 0), (FWD, CROSS, 0), (FWD, SEND, 0, 1), (FWD, RELAY, 0, 0), (FWD, NEAR, 0),
    (FWD, CROSS, 1), (FWD, RELAY, 0, 1), (FWD, WORK, 0, 0), (FWD, TOK, 0, 0, 1), (FWD, NORM, 0),
    (FWD, FAR, 0), (FWD, SEND, 1, 0), (FWD, NEAR, 1), (FWD, TOK, 0, 0, 2), (FWD, WORK, 0, 1),
    (FWD, TOK, 0, 1, 1), (FWD, SEND, 1, 1), (FWD, TOK, 0, 0, 3), (FWD, RELAY, 1, 0), (FWD, FAR, 1),
    (FWD, TOK, 0, 1, 2), (FWD, TOK, 0, 0, 4), (FWD, SEND, 3, 0), (FWD, RELAY, 1, 1),
    (FWD, TOK, 0, 1, 3), (FWD, WORK, 1, 0), (FWD, NORM, 1), (FWD, TOK, 1, 0, 1), (FWD, SEND, 3, 1),
    (FWD, TOK, 0, 0, 5), (FWD, RELAY, 3, 0), (FWD, TOK, 0, 1, 4), (FWD, WORK, 1, 1),
    (FWD, TOK, 0, 0, 6), (FWD, TOK, 1, 0, 2), (FWD, TOK, 1, 1, 1), (FWD, SEND, 2, 0),
    (FWD, RELAY, 3, 1), (FWD, TOK, 0, 0, 7), (FWD, TOK, 0, 1, 5), (FWD, WORK, 3, 0), (FWD, NORM, 2),
    (FWD, TOK, 1, 0, 3), (FWD, TOK, 3, 0, 1), (FWD, TOK, 1, 1, 2), (FWD, SEND, 2, 1),
    (FWD, RELAY, 2, 0), (FWD, TOK, 0, 1, 6), (FWD, WORK, 3, 1), (FWD, TOK, 0, 1, 7),
    (FWD, TOK, 1, 0, 4), (FWD, TOK, 1, 1, 3), (FWD, TOK, 3, 0, 2), (FWD, TOK, 3, 1, 1),
    (FWD, RELAY, 2, 1), (FWD, TOK, 1, 0, 5), (FWD, WORK, 2, 0), (FWD, TOK, 2, 0, 1),
    (FWD, TOK, 1, 1, 4), (FWD, TOK, 3, 1, 2), (FWD, TOK, 3, 0, 3), (FWD, TOK, 2, 0, 2),
    (FWD, TOK, 1, 0, 6), (FWD, TOK, 1, 1, 5), (FWD, WORK, 2, 1), (FWD, TOK, 1, 0, 7),
    (FWD, TOK, 3, 1, 3), (FWD, TOK, 2, 1, 1), (MID, BEGIN, 0, 0), (MID, BEGIN, 0, 1),
    (FWD, TOK, 3, 0, 4), (FWD, TOK, 2, 1, 2), (FWD, TOK, 2, 0, 3), (MID, RELAY, 0, 0),
    (MID, BEGIN, 1, 0), (FWD, TOK, 1, 1, 6), (FWD, TOK, 3, 1, 4), (MID, RELAY, 0, 1),
    (FWD, TOK, 3, 0, 5), (FWD, TOK, 1, 1, 7), (MID, BEGIN, 1, 1), (FWD, TOK, 2, 1, 3),
    (MID, REDUCE, 0, 0), (MID, RELAY, 1, 0), (FWD, TOK, 2, 0, 4), (FWD, TOK, 3, 1, 5),
    (MID, REDUCE, 0, 1), (FWD, TOK, 3, 0, 6), (MID, RELAY, 1, 1), (FWD, TOK, 2, 1, 4),
    (FWD, TOK, 3, 0, 7), (MID, BEGIN, 3, 0), (FWD, TOK, 3, 1, 6), (FWD, TOK, 2, 0, 5),
    (MID, REDUCE, 1, 0), (FWD, TOK, 2, 1, 5), (MID, REDUCE, 1, 1), (FWD, TOK, 3, 1, 7),
    (MID, BEGIN, 3, 1), (FWD, TOK, 2, 0, 6), (FWD, TOK, 2, 1, 6), (MID, RELAY, 3, 0),
    (FWD, TOK, 2, 0, 7), (MID, BEGIN, 2, 0), (FWD, TOK, 2, 1, 7), (MID, BEGIN, 2, 1),
    (MID, RELAY, 3, 1), (MID, REDUCE, 3, 0), (MID, RELAY, 2, 0), (MID, RELAY, 2, 1),
    (MID, REDUCE, 3, 1), (MID, REDUCE, 2, 0), (MID, REDUCE, 2, 1), (MID, JOIN, 0), (MID, JOIN, 1),
    (MID, FINISH, 0), (MID, FINISH, 1), (BWD, SEND, 0, 0), (BWD, CROSS, 0), (BWD, SEND, 0, 1),
    (BWD, RELAY, 0, 0), (BWD, NEAR, 0), (BWD, CROSS, 1), (BWD, RELAY, 0, 1), (BWD, WORK, 0, 0),
    (BWD, TOK, 0, 0, 1), (BWD, FAR, 0), (BWD, SEND, 1, 0), (BWD, TOK, 0, 0, 2), (BWD, NEAR, 1),
    (BWD, WORK, 0, 1), (BWD, TOK, 0, 0, 3), (BWD, TOK, 0, 1, 1), (BWD, SEND, 1, 1),
    (BWD, RELAY, 1, 0), (BWD, TOK, 0, 0, 4), (BWD, TOK, 0, 1, 2), (BWD, FAR, 1), (BWD, SEND, 3, 0),
    (BWD, TOK, 0, 0, 5), (BWD, RELAY, 1, 1), (BWD, TOK, 0, 1, 3), (BWD, WORK, 1, 0),
    (BWD, TOK, 0, 0, 6), (BWD, TOK, 1, 0, 1), (BWD, TOK, 0, 1, 4), (BWD, SEND, 3, 1),
    (BWD, RELAY, 3, 0), (BWD, TOK, 0, 0, 7), (BWD, TOK, 1, 0, 2), (BWD, WORK, 1, 1),
    (BWD, TOK, 0, 1, 5), (BWD, TOK, 1, 1, 1), (BWD, SEND, 2, 0), (BWD, TOK, 1, 0, 3),
    (BWD, RELAY, 3, 1), (BWD, TOK, 0, 1, 6), (BWD, WORK, 3, 0), (BWD, TOK, 1, 0, 4),
    (BWD, TOK, 1, 1, 2), (BWD, TOK, 0, 1, 7), (BWD, TOK, 3, 0, 1), (BWD, SEND, 2, 1),
    (BWD, RELAY, 2, 0), (BWD, WORK, 3, 1), (BWD, TOK, 1, 0, 5), (BWD, TOK, 1, 1, 3),
    (BWD, TOK, 3, 0, 2), (BWD, TOK, 3, 1, 1), (BWD, RELAY, 2, 1), (BWD, TOK, 1, 0, 6),
    (BWD, TOK, 1, 1, 4), (BWD, WORK, 2, 0), (BWD, TOK, 1, 0, 7), (BWD, TOK, 3, 0, 3),
    (BWD, TOK, 3, 1, 2), (BWD, TOK, 2, 0, 1), (BWD, TOK, 1, 1, 5), (BWD, WORK, 2, 1),
    (BWD, TOK, 3, 0, 4), (BWD, TOK, 3, 1, 3), (BWD, TOK, 2, 0, 2), (BWD, TOK, 2, 1, 1),
    (BWD, TOK, 1, 1, 6), (BWD, TOK, 3, 0, 5), (BWD, TOK, 3, 1, 4), (BWD, TOK, 2, 1, 2),
    (BWD, TOK, 1, 1, 7), (BWD, TOK, 2, 0, 3), (BWD, TOK, 3, 0, 6), (BWD, TOK, 3, 1, 5),
    (BWD, TOK, 3, 0, 7), (BWD, TOK, 2, 1, 3), (BWD, TOK, 2, 0, 4), (BWD, TOK, 3, 1, 6),
    (BWD, TOK, 2, 1, 4), (BWD, TOK, 3, 1, 7), (BWD, TOK, 2, 0, 5), (BWD, TOK, 2, 1, 5),
    (BWD, TOK, 2, 0, 6), (BWD, TOK, 2, 1, 6), (BWD, TOK, 2, 0, 7), (BWD, TOK, 2, 1, 7),
)


class Flow:
    def __init__(self, h):
        x, y = plane()
        self.h = h
        self.p, self.q = (x, y) if h == 0 else (y, x)

    def near(self, dp, dq):
        p, q = ring(self.p, dp), ring(self.q, dq)
        return lat_peer(q, p) if self.h == 0 else lat_peer(p, q)

    def unit(self, dq):
        return self.h * SIDE + ring(self.q, dq)


class Gather:
    def __init__(self, wires, flows, tag, own, held):
        self.wires, self.flows, self.tag, self.own, self.held = wires, flows, tag, own, held

    def p1(self, f, e, d):
        dst = self.held.at[1 if d == 1 else 3, f.unit(0), piece(e)]
        return self.wires.copy(("p1", f.h, e, d), self.own(f.h, e), dst, f.near(d, 0))

    def p1half(self, f, e, d):
        src = self.held.at[1 if d == 1 else 3, f.unit(0), rows_of(d, e)]
        dst = self.held.at[2, f.unit(0), rows_of(d, e)]
        return self.wires.copy(("p1half", f.h, e, d), src, dst, f.near(d, 0))

    def p2(self, f, k, e, d):
        at = self.held.at[k, f.unit(0), piece(e)]
        return self.wires.copy(("p2", f.h, k, e, d), self.own(f.h, e) if k == 0 else at, at, f.near(0, d))

    def p2half(self, f, k, e, d):
        at = self.held.at[k, f.unit(-d), rows_of(d, e)]
        return self.wires.copy(("p2half", f.h, k, e, d), at, at, f.near(0, d))

    def name(self, k):
        return (self.tag, k)

    def each(self, make, *where):
        for f in self.flows:
            for d in DIRS:
                yield make(f, *where, d)

    def send(self, k, e):
        for copy in self.each(self.p2, k, e):
            self.wires.go(copy, self.name(k))

    def cross(self, e):
        for copy in self.each(self.p1, e):
            self.wires.go(copy, self.name(0))

    def near(self, e):
        for copy in self.each(self.p1, e):
            copy.wait_recv()
        for f in self.flows:
            for d, k in ((1, 1), (-1, 3)):
                self.wires.go(self.p1half(f, e, d), self.name(k))

    def far(self, e):
        for copy in self.each(self.p1half, e):
            copy.wait_recv()

    def relay(self, k, e):
        for f in self.flows:
            for d in DIRS:
                self.p2(f, k, e, d).wait_recv()
                self.wires.go(self.p2half(f, k, e, d), self.name(k))

    def complete(self, k, e):
        for copy in self.each(self.p2half, k, e):
            copy.wait_recv()


def tok_flow(wires, tag, k, e, part, out, r1, s1, r2, r3, epilogue):
    n = ORDER.index((k, e)) % SLOTS
    z, core = column()
    other = tok_peer(z, 1 - core)
    me = core * SIDE + z
    source = (tag, k, e)

    def peer(d):
        return tok_peer(ring(z, d), core)

    def swap(j):
        at = ring(z, j)
        return wires.copy(("tok", k, e, 0, j), part.at[n, (1 - core) * SIDE + at], r1.at[n, j], other)

    def far(d):
        return wires.copy(("tok", k, e, 1, d), s1.at[n, 2, rows_of(d)], r2.at[n, s(d)], peer(d))

    def plain(d):
        src = s1.at[n, 1 if d == 1 else 3, rows_of(-d)]
        return wires.copy(("tok", k, e, 2, d), src, r3.at[n, s(d), rows_of(-d)], peer(d))

    def summed(d):
        src = s1.at[n, 1 if d == 1 else 3, rows_of(d)]
        return wires.copy(("tok", k, e, 3, d), src, r3.at[n, s(d), rows_of(d)], peer(d))

    def spread(d):
        at = out.at[k, me, piece(e)]
        return wires.copy(("tok", k, e, 4, d), at, at, peer(d))

    def forward(d):
        at = out.at[k, core * SIDE + ring(z, -d), rows_of(d, e)]
        return wires.copy(("tok", k, e, 5, d), at, at, peer(d))

    def hand(j):
        at = out.at[k, core * SIDE + ring(z, j), piece(e)]
        return wires.copy(("tok", k, e, 6, j), at, at, other)

    def first(j):
        swap(j).wait_recv()
        at = core * SIDE + ring(z, j)
        s1[n, j] = (f32(part[n, at]) + f32(r1[n, j])).astype(s1.dtype)

    for j in (2, 1, 3, 0):
        wires.go(swap(j), source)
    yield
    first(2)
    for d in DIRS:
        wires.go(far(d), source)
    for d in DIRS:
        first(1 if d == 1 else 3)
        wires.go(plain(d), source)
    first(0)
    yield
    for d in DIRS:
        far(d).wait_recv()
        j = 1 if d == 1 else 3
        s1[n, j, rows_of(d)] = (f32(s1[n, j, rows_of(d)]) + f32(r2[n, s(d)])).astype(s1.dtype)
        wires.go(summed(d), source)
    yield
    for d in DIRS:
        plain(d).wait_recv()
        summed(d).wait_recv()
    total = f32(s1[n, 0]) + f32(r3[n, 0]) + f32(r3[n, 1])
    out[k, me, piece(e)] = epilogue(k, e, me, total).astype(out.dtype)
    for d in DIRS:
        wires.go(spread(d))
    wires.go(hand(0))
    yield
    for d in DIRS:
        spread(d).wait_recv()
        wires.go(forward(d))
        wires.go(hand(3 if d == 1 else 1))
    hand(0).wait_recv()
    wires.settle(source)
    yield
    for d in DIRS:
        forward(d).wait_recv()
    wires.go(hand(2))
    yield
    for j in range(1, SIDE):
        hand(j).wait_recv()
    yield


def tok_buffers(dtype, width):
    return [
        pltpu.VMEM((SLOTS, 2 * SIDE, PIECE, width), dtype),
        pltpu.VMEM((SLOTS, SIDE, PIECE, width), dtype),
        pltpu.VMEM((SLOTS, SIDE, PIECE, width), dtype),
        pltpu.VMEM((SLOTS, 2, HALF, width), dtype),
        pltpu.VMEM((SLOTS, 2, PIECE, width), dtype),
    ]


def blocks(count, body):
    def step(i, carry):
        body(i)
        return carry

    lax.fori_loop(0, count, step, 0)


def own_tile(k):
    x, y = plane()
    z, core = column()
    return (1 - core) * (z * SIDE + ring(x, -k)) + core * (ring(y, -k) * SIDE + z)


ALL = 2 * SIDE * PIECE


def step_kernel(
    scale,
    x,
    enc_in,
    dec_in,
    enc_bias,
    dec_bias,
    mask,
    sq,
    xs,
    es,
    feat_out,
    grad_out,
    sq_sum,
    enc,
    dec,
    held,
    err,
    feats,
    grads,
    r1,
    r2,
    r4,
    r5,
    norm,
    sq_a,
    sq_b,
    *rest,
):
    fwd, bwd, (local, send, recv) = rest[:5], rest[5:10], rest[10:]
    wires = Wires(send, recv)
    z, core = column()
    flows = [Flow(h) for h in FLOWS]
    slab_count, depth, block = enc.shape
    width = dec.shape[0]
    cols = 512
    loads = [
        pltpu.make_async_copy(enc_in, enc, local.at[18]),
        pltpu.make_async_copy(dec_in, dec, local.at[19]),
    ]
    keep = [pltpu.make_async_copy(x.at[f.h], held.at[0, f.unit(0)], local.at[f.h]) for f in flows]
    saves = {}

    def save(name, k, src, dst):
        n = 2 + len(saves)
        saves[name, k] = pltpu.make_async_copy(src.at[k], dst.at[k], local.at[n])
        saves[name, k].start()

    for copy in keep:
        copy.start()
    for copy in loads:
        copy.start()
    greet()


    def feature(k, e, me, total):
        live = mask[own_tile(k)] > 0.0
        return jnp.where(live, jnp.maximum(total + enc_bias[...], 0.0), 0.0)

    def encode(k, e):
        n = ORDER.index((k, e)) % SLOTS
        if (k, e) == ORDER[0]:
            for copy in keep + loads:
                copy.wait()

        def step(slab):
            rows = held[k, :, piece(e)].reshape(ALL, depth)
            at = pl.ds(pl.multiple_of(slab * block, block), block)
            value = jnp.dot(rows, enc[slab], preferred_element_type=F32)
            fwd[0][n, :, :, at] = value.reshape(2 * SIDE, PIECE, block)

        blocks(slab_count, step)
        if e == PIECES[-1]:
            save("x", k, held, xs)

    swap = wires.copy("sq", sq, sq_a.at[0], tok_peer(z, 1 - core))
    turns = [wires.copy(("sq", d), sq_b.at[0], sq_b.at[1 + s(d)], tok_peer(ring(z, d), core)) for d in DIRS]
    turn_on = wires.copy(("sq", 2), sq_b.at[1], sq_b.at[3], tok_peer(ring(z, 1), core))

    def norms(stage):
        if stage == 0:
            swap.wait_recv()
            sq_b[0] = sq[...] + sq_a[0]
            for copy in turns:
                wires.go(copy)
        elif stage == 1:
            for copy in turns:
                copy.wait_recv()
            wires.go(turn_on)
        else:
            turn_on.wait_recv()
            total = (sq_b[0] + sq_b[3]) + (sq_b[1] + sq_b[2])
            sq_sum[...] = total
            norm[...] = jnp.sum(jnp.sqrt(total + NORM_EPSILON), axis=0, keepdims=True)

    wires.go(swap)


    def decode(k, e):
        if e == PIECES[0]:
            wires.settle(front.name(k))
            saves["x", k].wait()

        def step(col):
            at = pl.ds(pl.multiple_of(col * cols, cols), cols)
            f = feats[k, :, piece(e)].reshape(ALL, width)
            value = jnp.dot(f, dec[:, at], preferred_element_type=F32)
            held[k, :, piece(e), at] = value.reshape(2 * SIDE, PIECE, cols).astype(BF16)

        blocks(depth // cols, step)

    def half(d, e):
        return pl.ds(e * HALF, HALF)

    def far(f, k, e, d):
        src = held.at[k, f.unit(2), rows_of(d, e)]
        return wires.copy((0, f.h, k, e, d), src, r1.at[f.h, k, s(d), half(d, e)], f.near(0, d))

    def plain(f, k, e, d):
        src = held.at[k, f.unit(d), rows_of(-d, e)]
        return wires.copy((1, f.h, k, e, d), src, r2.at[f.h, k, s(d), rows_of(-d, e)], f.near(0, d))

    def summed(f, k, e, d):
        src = held.at[k, f.unit(d), rows_of(d, e)]
        return wires.copy((2, f.h, k, e, d), src, r2.at[f.h, k, s(d), rows_of(d, e)], f.near(0, d))

    def far2(f, e, d):
        src = held.at[2, f.unit(0), rows_of(d, e)]
        return wires.copy((3, f.h, e, d), src, r4.at[f.h, s(d), half(d, e)], f.near(d, 0))

    def plain2(f, e, d):
        src = held.at[3 if d == 1 else 1, f.unit(0), rows_of(-d, e)]
        return wires.copy((4, f.h, e, d), src, r5.at[f.h, s(d), rows_of(-d, e)], f.near(d, 0))

    def summed2(f, e, d):
        src = held.at[3 if d == 1 else 1, f.unit(0), rows_of(d, e)]
        return wires.copy((5, f.h, e, d), src, r5.at[f.h, s(d), rows_of(d, e)], f.near(d, 0))

    def reduce_begin(k, e):
        decode(k, e)
        for make in (far, plain):
            for f in flows:
                for d in DIRS:
                    wires.go(make(f, k, e, d))

    def reduce_relay(k, e):
        for f in flows:
            for d in DIRS:
                far(f, k, e, d).wait_recv()
                at = (k, f.unit(d), rows_of(d, e))
                held[at] = (f32(held[at]) + f32(r1[f.h, k, s(d), half(d, e)])).astype(BF16)
                wires.go(summed(f, k, e, d))

    def reduce(k, e):
        for f in flows:
            for d in DIRS:
                plain(f, k, e, d).wait_recv()
                summed(f, k, e, d).wait_recv()
            at = (k, f.unit(0), piece(e))
            total = f32(held[at]) + f32(r2[f.h, k, 0, piece(e)]) + f32(r2[f.h, k, 1, piece(e)])
            held[at] = total.astype(BF16)
            if k == 2:
                for d in DIRS:
                    wires.go(far2(f, e, d))
            elif k != 0:
                wires.go(plain2(f, e, 1 if k == 3 else -1))

    def reduce_far(e):
        for f in flows:
            for d in DIRS:
                far2(f, e, d).wait_recv()
                at = (3 if d == 1 else 1, f.unit(0), rows_of(d, e))
                held[at] = (f32(held[at]) + f32(r4[f.h, s(d), half(d, e)])).astype(BF16)
                wires.go(summed2(f, e, d))

    def finish(e):
        for f in flows:
            for d in DIRS:
                plain2(f, e, d).wait_recv()
                summed2(f, e, d).wait_recv()
            at = f.unit(0), piece(e)
            recon = f32(held[(0,) + at]) + f32(r5[f.h, 0, piece(e)]) + f32(r5[f.h, 1, piece(e)]) + dec_bias[...]
            err[(0,) + at] = (recon - f32(x[f.h, piece(e)])).astype(BF16)
        if e == PIECES[-1]:
            wires.drain()


    def project(k, e):
        n = ORDER.index((k, e)) % SLOTS

        def step(slab):
            at = pl.ds(pl.multiple_of(slab * block, block), block)
            rows = err[k, :, piece(e)].reshape(ALL, depth)
            value = lax.dot_general(rows, dec[at], NT, preferred_element_type=F32)
            bwd[0][n, :, :, at] = value.reshape(2 * SIDE, PIECE, block).astype(BF16)

        blocks(slab_count, step)
        if e == PIECES[-1]:
            save("e", k, err, es)

    def pre_grad(k, e, me, total):
        grad = scale * (total + SPARSITY * norm[...])
        return jnp.where(f32(feats[k, me, piece(e)]) > 0.0, grad, 0.0)

    front = Gather(wires, flows, "x", lambda h, e: x.at[h, piece(e)], held)
    back = Gather(wires, flows, "e", lambda h, e: err.at[0, flows[h].unit(0), piece(e)], err)
    toks = {
        FWD: {g: tok_flow(wires, FWD, *g, fwd[0], feats, *fwd[1:], feature) for g in ORDER},
        BWD: {g: tok_flow(wires, BWD, *g, bwd[0], grads, *bwd[1:], pre_grad) for g in ORDER},
    }

    def tok(phase, k, e, number):
        next(toks[phase][k, e])
        if number == 7 and e == PIECES[-1]:
            save(phase, k, *((feats, feat_out) if phase == FWD else (grads, grad_out)))

    steps = {MID: {BEGIN: reduce_begin, RELAY: reduce_relay, REDUCE: reduce, JOIN: reduce_far, FINISH: finish}}
    for phase, g, work in ((FWD, front, encode), (BWD, back, project)):
        steps[phase] = {SEND: g.send, CROSS: g.cross, NEAR: g.near, FAR: g.far, RELAY: g.relay, NORM: norms}
        steps[phase][TOK] = functools.partial(tok, phase)

        def arrive(k, e, g=g, work=work):
            g.complete(k, e)
            work(k, e)

        steps[phase][WORK] = arrive
    for phase, what, *where in SCRIPT:
        steps[phase][what](*where)
    for (name, _), copy in saves.items():
        if name != "x":
            copy.wait()
    wires.drain()


VMEM = pl.BlockSpec(memory_space=pltpu.VMEM)
ANY = pl.BlockSpec(memory_space=pl.ANY)


def step(scale, x, enc, dec, enc_bias, dec_bias, mask, sq):
    width, depth = dec.shape
    units = (SIDE, 2 * SIDE, UNIT)
    rows = jax.ShapeDtypeStruct(units + (depth,), BF16)
    latents = jax.ShapeDtypeStruct(units + (width,), BF16)
    return pl.pallas_call(
        functools.partial(step_kernel, scale),
        out_shape=[rows, rows, latents, latents, jax.ShapeDtypeStruct(sq.shape, F32)],
        in_specs=[VMEM, ANY, ANY] + [VMEM] * 4,
        out_specs=[ANY, ANY, ANY, ANY, VMEM],
        scratch_shapes=[
            pltpu.VMEM(enc.shape, BF16),
            pltpu.VMEM(dec.shape, BF16),
            pltpu.VMEM(units + (depth,), BF16),
            pltpu.VMEM(units + (depth,), BF16),
            pltpu.VMEM(units + (width,), BF16),
            pltpu.VMEM(units + (width,), BF16),
            pltpu.VMEM((2, SIDE, 2, UNIT // 2, depth), BF16),
            pltpu.VMEM((2, SIDE, 2, UNIT, depth), BF16),
            pltpu.VMEM((2, 2, UNIT // 2, depth), BF16),
            pltpu.VMEM((2, 2, UNIT, depth), BF16),
            pltpu.VMEM((1, width), F32),
            pltpu.VMEM((1,) + sq.shape, F32),
            pltpu.VMEM((4,) + sq.shape, F32),
        ]
        + tok_buffers(F32, width)
        + tok_buffers(BF16, width)
        + [
            pltpu.SemaphoreType.DMA((20,)),
            pltpu.SemaphoreType.DMA((348,)),
            pltpu.SemaphoreType.DMA((348,)),
        ],
        compiler_params=pltpu.CompilerParams(
            vmem_limit_bytes=60 * 1024 * 1024, collective_id=0, has_side_effects=True
        ),
        name="step",
    )(x, enc, dec, enc_bias, dec_bias, mask, sq)


QUAD = 4


def weights_kernel(
    scale, units, count, x0, x1, e0, e1, feats, grads, d0, d1, inv_norm, grad_enc, grad_dec, enc_sum, err_sum, acc_e, acc_d, tot, gsum, mixed
):
    slabs, block = grad_enc.shape[0], grad_enc.shape[3]
    for m, err in enumerate((e0, e1)):
        rows = err[...].reshape(-1, err.shape[2])
        ones = jnp.ones((16, rows.shape[0]), BF16)
        total = jnp.dot(ones, rows, preferred_element_type=F32)
        err_sum[pl.ds(m, 1)] = scale * total[:1]
    for slab in range(slabs):
        at = pl.ds(slab * block, block)
        acc_e[...] = jnp.zeros_like(acc_e)
        acc_d[...] = jnp.zeros_like(acc_d)
        tot[...] = jnp.zeros_like(tot)
        gsum[...] = jnp.zeros_like(gsum)

        def pair(i, carry, slab=slab, at=at):
            ids = [units[slab * 2 * MOST + i * QUAD + n] for n in range(QUAD)]
            f = jnp.concatenate([feats[n, :, at] for n in ids], axis=0)
            g = jnp.concatenate([grads[n, :, at] for n in ids], axis=0)
            for m, (acts, err) in enumerate(((x0, e0), (x1, e1))):
                a = jnp.concatenate([acts[n] for n in ids], axis=0)
                e = jnp.concatenate([err[n] for n in ids], axis=0)
                acc_e[m] += lax.dot_general(a, g, TN, preferred_element_type=F32)
                acc_d[m] += lax.dot_general(f, e, TN, preferred_element_type=F32)
            tot[...] += lax.dot_general(f, jnp.ones((QUAD * UNIT, 128), BF16), TN, preferred_element_type=F32)
            gsum[...] += jnp.dot(jnp.ones((16, QUAD * UNIT), BF16), g, preferred_element_type=F32)
            return carry

        lax.fori_loop(0, lax.div(count[slab] + 1, 2), pair, 0)
        enc_sum[:, at] = gsum[:8]
        both = []
        for m, dec in enumerate((d0, d1)):
            grad_enc[slab, m] = acc_e[m].astype(grad_enc.dtype)
            col = SPARSITY * tot[:, :1] * inv_norm[m, at, :]
            both.append(scale * (acc_d[m] + col * f32(dec[at])))
        for m in range(len(both)):
            mixed[:, m, :] = both[m]
        grad_dec[at] = mixed[...].astype(grad_dec.dtype)


def weights(scale, units, count, xs, es, feats, grads, dec, inv_norm, models, slabs):
    width, depth = dec.shape
    cols = 256
    block = width // slabs
    part = depth // models
    steps = part // cols

    def whole(a):
        return pl.BlockSpec(a.shape, lambda c, *_: (0,) * a.ndim)

    def wide(a, m):
        return pl.BlockSpec(a.shape[:-1] + (cols,), lambda c, *_: (0,) * (a.ndim - 1) + (c + m * steps,))

    return pl.pallas_call(
        functools.partial(weights_kernel, scale),
        out_shape=[
            jax.ShapeDtypeStruct((slabs, models, part, block), BF16),
            jax.ShapeDtypeStruct((width, models, part), BF16),
            jax.ShapeDtypeStruct((8, width), F32),
            jax.ShapeDtypeStruct((models, part), F32),
        ],
        grid_spec=pltpu.PrefetchScalarGridSpec(
            num_scalar_prefetch=2,
            grid=(steps,),
            in_specs=[
                wide(xs, 0),
                wide(xs, 1),
                wide(es, 0),
                wide(es, 1),
                whole(feats),
                whole(grads),
                wide(dec, 0),
                wide(dec, 1),
                whole(inv_norm),
            ],
            out_specs=[
                pl.BlockSpec((slabs, models, cols, block), lambda c, *_: (0, 0, c, 0)),
                pl.BlockSpec((width, models, cols), lambda c, *_: (0, 0, c)),
                pl.BlockSpec((8, width), lambda c, *_: (0, 0)),
                pl.BlockSpec((models, cols), lambda c, *_: (0, c)),
            ],
            scratch_shapes=[
                pltpu.VMEM((models, cols, block), F32),
                pltpu.VMEM((models, block, cols), F32),
                pltpu.VMEM((block, 128), F32),
                pltpu.VMEM((16, block), F32),
                pltpu.VMEM((block, models, cols), F32),
            ],
        ),
        compiler_params=pltpu.CompilerParams(vmem_limit_bytes=56 * 1024 * 1024),
        name="weights",
    )(units, count, xs, xs, es, es, feats, grads, dec, dec, inv_norm)


def unit_lists(is_active):
    tiles = is_active.shape[0]
    ids = jnp.arange(tiles, dtype=jnp.int32)
    before = (ids[:, None] > ids[None, :]).astype(jnp.int32)
    rank = jnp.sum(before[:, :, None] * is_active[None], axis=1)
    places = jnp.arange(MOST, dtype=jnp.int32)
    picked = (is_active[:, :, None] == 1) & (rank[:, :, None] == places)
    idle = jnp.min(jnp.where(is_active == 0, ids[:, None], tiles - 1), axis=0)
    count = jnp.sum(is_active, axis=0)
    tile = jnp.sum(jnp.where(picked, ids[:, None, None], 0), axis=0)
    tile = jnp.where(places[None, :] < count[:, None], tile, idle[:, None])
    x, y = plane()
    tx, ty = tile % SIDE, tile // SIDE
    one = ((x - tx) % SIDE) * 2 * SIDE + ty
    two = ((y - ty) % SIDE) * 2 * SIDE + SIDE + tx
    return jnp.stack([one, two], axis=2).reshape(-1), count


def on_device(activations, enc_weight, enc_bias, dec_weight, dec_bias, active):
    slabs, models, depth, block = enc_weight.shape
    rows, tiles = activations.shape[0], active.shape[0]
    width = slabs * block
    scale = 1.0 / math.sqrt(MOST * TILE)
    ids = lax.axis_index("lat") * slabs + jnp.arange(slabs, dtype=jnp.int32)
    is_active = jnp.any(active[:, :, None] == ids[None, None, :], axis=1).astype(jnp.int32)
    mask = jnp.broadcast_to(is_active.astype(F32)[:, None, :, None], (tiles, 1, slabs, block))
    mask = mask.reshape(tiles, 1, width)
    units, count = unit_lists(is_active)
    x = activations.reshape(2, rows // 2, models * depth)
    dec = dec_weight.reshape(width, models * depth)
    sq = jnp.stack(
        [jnp.sum(jnp.square(dec[:, m * depth : (m + 1) * depth].astype(F32)), axis=1) for m in range(models)]
    )
    enc = enc_weight.reshape(slabs, models * depth, block)
    xs, es, feats, grads, sq_sum = step(
        scale, x, enc, dec, enc_bias.reshape(1, width), dec_bias.reshape(1, models * depth), mask, sq
    )
    inv_norm = (1.0 / jnp.sqrt(sq_sum + NORM_EPSILON))[:, :, None]
    flat = (2 * tiles, UNIT)
    grad_enc, grad_dec, enc_sum, err_sum = weights(
        scale,
        units,
        count,
        xs.reshape(flat + (models * depth,)),
        es.reshape(flat + (models * depth,)),
        feats.reshape(flat + (width,)),
        grads.reshape(flat + (width,)),
        dec,
        inv_norm,
        models,
        slabs,
    )
    return (
        grad_enc,
        enc_sum[0].reshape(slabs, block),
        grad_dec.reshape(dec_weight.shape),
        err_sum,
    )


def solution(mesh):
    placed = (
        P("lat", None, "tok"),
        P("lat", None, "tok", None),
        P("lat", None),
        P("lat", None, None, "tok"),
        P(None, "tok"),
        P(),
    )
    return jax.shard_map(
        on_device,
        mesh=mesh,
        in_specs=placed,
        out_specs=(
            P("lat", None, "tok", None),
            P("lat", None),
            P("lat", None, None, "tok"),
            P(None, "tok"),
        ),
        check_vma=False,
    )
```

```python
import functools
import math

import jax
import jax.numpy as jnp
from jax import lax
from jax.experimental import pallas as pl
from jax.experimental.pallas import tpu as pltpu
from jax.sharding import PartitionSpec as P

MOST = 8
TILE = 128
SPARSITY = 0.25
NORM_EPSILON = 1e-06
MESH = pl.DeviceIdType.MESH
SIDE = 4
UNIT = TILE // 2
PIECE = UNIT // 2
HALF = PIECE // 2
PIECES = (0, 1)
SLOTS = 4
DIRS = (1, -1)
ORDER = tuple((k, e) for k in (0, 1, 3, 2) for e in PIECES)
BF16, F32 = jnp.bfloat16, jnp.float32
NT = (((1,), (1,)), ((), ()))
TN = (((0,), (0,)), ((), ()))


def ring(i, step):
    return lax.rem(i + step + SIDE, SIDE)


def lat_peer(y, x):
    return {"lat": y * SIDE + x}


def tok_peer(z, core):
    return {"tok": z * 2 + core}


def plane():
    lat = lax.axis_index("lat")
    return lax.rem(lat, SIDE), lax.div(lat, SIDE)


def column():
    tok = lax.axis_index("tok")
    return lax.div(tok, 2), lax.rem(tok, 2)


def greet():
    x, y = plane()
    z, core = column()
    peers = [lat_peer(y, ring(x, d)) for d in DIRS] + [lat_peer(ring(y, d), x) for d in DIRS]
    peers += [tok_peer(ring(z, d), core) for d in DIRS] + [tok_peer(z, 1 - core)]
    barrier = pltpu.get_barrier_semaphore()
    for peer in peers:
        pl.semaphore_signal(barrier, inc=1, device_id=peer, device_id_type=MESH)
    pl.semaphore_wait(barrier, len(peers))


def s(d):
    return 0 if d == 1 else 1


def rows_of(d, e=0):
    return pl.ds(e * PIECE + (0 if d == 1 else HALF), HALF)


def piece(e):
    return pl.ds(e * PIECE, PIECE)


def f32(v):
    return v.astype(F32)


class Wires:
    def __init__(self, send, recv):
        self.send, self.recv = send, recv
        self.numbers, self.started = {}, []

    def copy(self, key, src, dst, peer):
        n = self.numbers.setdefault(key, len(self.numbers))
        return pltpu.make_async_remote_copy(
            src_ref=src,
            dst_ref=dst,
            send_sem=self.send.at[n],
            recv_sem=self.recv.at[n],
            device_id=peer,
            device_id_type=MESH,
        )

    def go(self, copy, source=None):
        copy.start()
        self.started.append((source, copy))

    def settle(self, source):
        for name, copy in self.started:
            if name == source:
                copy.wait_send()
        self.started = [item for item in self.started if item[0] != source]

    def drain(self):
        for _, copy in self.started:
            copy.wait_send()
        self.started = []


FLOWS = (0, 1)
FWD, MID, BWD = range(3)
SEND, CROSS, NEAR, FAR, RELAY, WORK, TOK, NORM, BEGIN, REDUCE, JOIN, FINISH = range(12)
SCRIPT = (
    (FWD, SEND, 0, 0), (FWD, CROSS, 0), (FWD, SEND, 0, 1), (FWD, RELAY, 0, 0), (FWD, NEAR, 0),
    (FWD, CROSS, 1), (FWD, RELAY, 0, 1), (FWD, WORK, 0, 0), (FWD, TOK, 0, 0, 1), (FWD, NORM, 0),
    (FWD, FAR, 0), (FWD, SEND, 1, 0), (FWD, NEAR, 1), (FWD, TOK, 0, 0, 2), (FWD, WORK, 0, 1),
    (FWD, TOK, 0, 1, 1), (FWD, SEND, 1, 1), (FWD, TOK, 0, 0, 3), (FWD, RELAY, 1, 0), (FWD, FAR, 1),
    (FWD, TOK, 0, 1, 2), (FWD, TOK, 0, 0, 4), (FWD, RELAY, 1, 1), (FWD, TOK, 0, 1, 3),
    (FWD, WORK, 1, 0), (FWD, NORM, 1), (FWD, SEND, 3, 0), (FWD, TOK, 1, 0, 1), (FWD, SEND, 3, 1),
    (FWD, WORK, 1, 1), (FWD, TOK, 1, 1, 1), (FWD, SEND, 2, 0), (FWD, TOK, 0, 0, 5),
    (FWD, TOK, 0, 1, 4), (FWD, TOK, 1, 0, 2), (FWD, RELAY, 3, 0), (FWD, TOK, 0, 0, 6),
    (FWD, TOK, 1, 1, 2), (FWD, TOK, 0, 1, 5), (FWD, TOK, 0, 0, 7), (FWD, RELAY, 3, 1),
    (FWD, TOK, 1, 0, 3), (FWD, SEND, 2, 1), (FWD, RELAY, 2, 0), (FWD, TOK, 1, 1, 3),
    (FWD, WORK, 3, 0), (FWD, NORM, 2), (FWD, TOK, 3, 0, 1), (FWD, TOK, 0, 1, 6), (FWD, WORK, 3, 1),
    (FWD, TOK, 1, 0, 4), (FWD, TOK, 3, 1, 1), (FWD, TOK, 1, 1, 4), (FWD, RELAY, 2, 1),
    (FWD, TOK, 3, 0, 2), (FWD, TOK, 0, 1, 7), (FWD, TOK, 1, 0, 5), (FWD, WORK, 2, 0),
    (FWD, TOK, 3, 1, 2), (FWD, TOK, 2, 0, 1), (FWD, TOK, 1, 1, 5), (FWD, WORK, 2, 1),
    (MID, BEGIN, 0, 1), (FWD, TOK, 1, 0, 6), (MID, BEGIN, 0, 0), (FWD, TOK, 3, 1, 3),
    (FWD, TOK, 1, 0, 7), (FWD, TOK, 2, 0, 2), (MID, BEGIN, 1, 0), (FWD, TOK, 1, 1, 6),
    (MID, RELAY, 0, 1), (FWD, TOK, 3, 1, 4), (MID, RELAY, 0, 0), (FWD, TOK, 2, 0, 3),
    (FWD, TOK, 1, 1, 7), (MID, BEGIN, 1, 1), (FWD, TOK, 3, 0, 3), (FWD, TOK, 2, 1, 1),
    (MID, RELAY, 1, 0), (FWD, TOK, 3, 1, 5), (FWD, TOK, 2, 0, 4), (MID, REDUCE, 0, 1),
    (FWD, TOK, 3, 0, 4), (FWD, TOK, 2, 1, 2), (FWD, TOK, 3, 1, 6), (MID, REDUCE, 0, 0),
    (FWD, TOK, 2, 0, 5), (MID, RELAY, 1, 1), (FWD, TOK, 3, 1, 7), (MID, BEGIN, 3, 1),
    (FWD, TOK, 3, 0, 5), (FWD, TOK, 2, 1, 3), (MID, REDUCE, 1, 0), (MID, REDUCE, 1, 1),
    (FWD, TOK, 2, 0, 6), (FWD, TOK, 3, 0, 6), (MID, RELAY, 3, 1), (FWD, TOK, 2, 0, 7),
    (MID, BEGIN, 2, 0), (FWD, TOK, 2, 1, 4), (FWD, TOK, 3, 0, 7), (MID, BEGIN, 3, 0),
    (MID, REDUCE, 3, 1), (FWD, TOK, 2, 1, 5), (MID, RELAY, 2, 0), (FWD, TOK, 2, 1, 6),
    (MID, RELAY, 3, 0), (FWD, TOK, 2, 1, 7), (MID, BEGIN, 2, 1), (MID, REDUCE, 2, 0),
    (MID, REDUCE, 3, 0), (MID, RELAY, 2, 1), (MID, JOIN, 0), (MID, REDUCE, 2, 1), (MID, FINISH, 0),
    (BWD, SEND, 0, 0), (BWD, CROSS, 0), (MID, JOIN, 1), (BWD, RELAY, 0, 0), (BWD, NEAR, 0),
    (MID, FINISH, 1), (BWD, SEND, 0, 1), (BWD, WORK, 0, 0), (BWD, TOK, 0, 0, 1), (BWD, CROSS, 1),
    (BWD, FAR, 0), (BWD, TOK, 0, 0, 2), (BWD, RELAY, 0, 1), (BWD, SEND, 1, 0), (BWD, TOK, 0, 0, 3),
    (BWD, NEAR, 1), (BWD, WORK, 0, 1), (BWD, TOK, 0, 1, 1), (BWD, TOK, 0, 0, 4), (BWD, SEND, 1, 1),
    (BWD, SEND, 3, 0), (BWD, RELAY, 1, 0), (BWD, TOK, 0, 1, 2), (BWD, FAR, 1), (BWD, TOK, 0, 0, 5),
    (BWD, TOK, 0, 1, 3), (BWD, RELAY, 1, 1), (BWD, TOK, 0, 0, 6), (BWD, TOK, 0, 1, 4),
    (BWD, TOK, 0, 0, 7), (BWD, RELAY, 3, 0), (BWD, WORK, 1, 0), (BWD, SEND, 3, 1),
    (BWD, TOK, 1, 0, 1), (BWD, TOK, 0, 1, 5), (BWD, WORK, 1, 1), (BWD, TOK, 1, 1, 1),
    (BWD, SEND, 2, 0), (BWD, WORK, 3, 0), (BWD, TOK, 1, 0, 2), (BWD, TOK, 3, 0, 1),
    (BWD, RELAY, 3, 1), (BWD, TOK, 1, 1, 2), (BWD, TOK, 0, 1, 6), (BWD, SEND, 2, 1),
    (BWD, TOK, 1, 0, 3), (BWD, TOK, 3, 0, 2), (BWD, TOK, 0, 1, 7), (BWD, RELAY, 2, 0),
    (BWD, TOK, 1, 1, 3), (BWD, WORK, 3, 1), (BWD, TOK, 1, 0, 4), (BWD, TOK, 3, 1, 1),
    (BWD, TOK, 3, 0, 3), (BWD, TOK, 1, 1, 4), (BWD, RELAY, 2, 1), (BWD, TOK, 3, 1, 2),
    (BWD, TOK, 1, 0, 5), (BWD, WORK, 2, 0), (BWD, TOK, 2, 0, 1), (BWD, TOK, 1, 1, 5),
    (BWD, TOK, 3, 0, 4), (BWD, TOK, 3, 1, 3), (BWD, WORK, 2, 1), (BWD, TOK, 2, 1, 1),
    (BWD, TOK, 2, 0, 2), (BWD, TOK, 1, 1, 6), (BWD, TOK, 1, 0, 6), (BWD, TOK, 3, 0, 5),
    (BWD, TOK, 2, 1, 2), (BWD, TOK, 1, 0, 7), (BWD, TOK, 2, 0, 3), (BWD, TOK, 1, 1, 7),
    (BWD, TOK, 3, 1, 4), (BWD, TOK, 3, 0, 6), (BWD, TOK, 2, 1, 3), (BWD, TOK, 3, 0, 7),
    (BWD, TOK, 2, 0, 4), (BWD, TOK, 3, 1, 5), (BWD, TOK, 2, 1, 4), (BWD, TOK, 2, 0, 5),
    (BWD, TOK, 3, 1, 6), (BWD, TOK, 2, 1, 5), (BWD, TOK, 3, 1, 7), (BWD, TOK, 2, 0, 6),
    (BWD, TOK, 2, 1, 6), (BWD, TOK, 2, 0, 7), (BWD, TOK, 2, 1, 7),
)


class Flow:
    def __init__(self, h):
        x, y = plane()
        self.h = h
        self.p, self.q = (x, y) if h == 0 else (y, x)

    def near(self, dp, dq):
        p, q = ring(self.p, dp), ring(self.q, dq)
        return lat_peer(q, p) if self.h == 0 else lat_peer(p, q)

    def unit(self, dq):
        return self.h * SIDE + ring(self.q, dq)


class Gather:
    def __init__(self, wires, flows, tag, own, held):
        self.wires, self.flows, self.tag, self.own, self.held = wires, flows, tag, own, held

    def p1(self, f, e, d):
        dst = self.held.at[1 if d == 1 else 3, f.unit(0), piece(e)]
        return self.wires.copy(("p1", f.h, e, d), self.own(f.h, e), dst, f.near(d, 0))

    def p1half(self, f, e, d):
        src = self.held.at[1 if d == 1 else 3, f.unit(0), rows_of(d, e)]
        dst = self.held.at[2, f.unit(0), rows_of(d, e)]
        return self.wires.copy(("p1half", f.h, e, d), src, dst, f.near(d, 0))

    def p2(self, f, k, e, d):
        at = self.held.at[k, f.unit(0), piece(e)]
        return self.wires.copy(("p2", f.h, k, e, d), self.own(f.h, e) if k == 0 else at, at, f.near(0, d))

    def p2half(self, f, k, e, d):
        at = self.held.at[k, f.unit(-d), rows_of(d, e)]
        return self.wires.copy(("p2half", f.h, k, e, d), at, at, f.near(0, d))

    def name(self, k):
        return (self.tag, k)

    def each(self, make, *where):
        for f in self.flows:
            for d in DIRS:
                yield make(f, *where, d)

    def send(self, k, e):
        for copy in self.each(self.p2, k, e):
            self.wires.go(copy, self.name(k))

    def cross(self, e):
        for copy in self.each(self.p1, e):
            self.wires.go(copy, self.name(0))

    def near(self, e):
        for copy in self.each(self.p1, e):
            copy.wait_recv()
        for f in self.flows:
            for d, k in ((1, 1), (-1, 3)):
                self.wires.go(self.p1half(f, e, d), self.name(k))

    def far(self, e):
        for copy in self.each(self.p1half, e):
            copy.wait_recv()

    def relay(self, k, e):
        for f in self.flows:
            for d in DIRS:
                self.p2(f, k, e, d).wait_recv()
                self.wires.go(self.p2half(f, k, e, d), self.name(k))

    def complete(self, k, e):
        for copy in self.each(self.p2half, k, e):
            copy.wait_recv()


def tok_flow(wires, tag, k, e, part, out, r1, s1, r2, r3, epilogue):
    n = ORDER.index((k, e)) % SLOTS
    z, core = column()
    other = tok_peer(z, 1 - core)
    me = core * SIDE + z
    source = (tag, k, e)

    def peer(d):
        return tok_peer(ring(z, d), core)

    def swap(j):
        at = ring(z, j)
        return wires.copy(("tok", k, e, 0, j), part.at[n, (1 - core) * SIDE + at], r1.at[n, j], other)

    def far(d):
        return wires.copy(("tok", k, e, 1, d), s1.at[n, 2, rows_of(d)], r2.at[n, s(d)], peer(d))

    def plain(d):
        src = s1.at[n, 1 if d == 1 else 3, rows_of(-d)]
        return wires.copy(("tok", k, e, 2, d), src, r3.at[n, s(d), rows_of(-d)], peer(d))

    def summed(d):
        src = s1.at[n, 1 if d == 1 else 3, rows_of(d)]
        return wires.copy(("tok", k, e, 3, d), src, r3.at[n, s(d), rows_of(d)], peer(d))

    def spread(d):
        at = out.at[k, me, piece(e)]
        return wires.copy(("tok", k, e, 4, d), at, at, peer(d))

    def forward(d):
        at = out.at[k, core * SIDE + ring(z, -d), rows_of(d, e)]
        return wires.copy(("tok", k, e, 5, d), at, at, peer(d))

    def hand(j):
        at = out.at[k, core * SIDE + ring(z, j), piece(e)]
        return wires.copy(("tok", k, e, 6, j), at, at, other)

    def first(j):
        swap(j).wait_recv()
        at = core * SIDE + ring(z, j)
        s1[n, j] = (f32(part[n, at]) + f32(r1[n, j])).astype(s1.dtype)

    for j in (2, 1, 3, 0):
        wires.go(swap(j), source)
    yield
    first(2)
    for d in DIRS:
        wires.go(far(d), source)
    for d in DIRS:
        first(1 if d == 1 else 3)
        wires.go(plain(d), source)
    first(0)
    yield
    for d in DIRS:
        far(d).wait_recv()
        j = 1 if d == 1 else 3
        s1[n, j, rows_of(d)] = (f32(s1[n, j, rows_of(d)]) + f32(r2[n, s(d)])).astype(s1.dtype)
        wires.go(summed(d), source)
    yield
    for d in DIRS:
        plain(d).wait_recv()
        summed(d).wait_recv()
    total = f32(s1[n, 0]) + f32(r3[n, 0]) + f32(r3[n, 1])
    out[k, me, piece(e)] = epilogue(k, e, me, total).astype(out.dtype)
    for d in DIRS:
        wires.go(spread(d))
    wires.go(hand(0))
    yield
    for d in DIRS:
        spread(d).wait_recv()
        wires.go(forward(d))
        wires.go(hand(3 if d == 1 else 1))
    hand(0).wait_recv()
    wires.settle(source)
    yield
    for d in DIRS:
        forward(d).wait_recv()
    wires.go(hand(2))
    yield
    for j in range(1, SIDE):
        hand(j).wait_recv()
    yield


def tok_buffers(dtype, width):
    return [
        pltpu.VMEM((SLOTS, 2 * SIDE, PIECE, width), dtype),
        pltpu.VMEM((SLOTS, SIDE, PIECE, width), dtype),
        pltpu.VMEM((SLOTS, SIDE, PIECE, width), dtype),
        pltpu.VMEM((SLOTS, 2, HALF, width), dtype),
        pltpu.VMEM((SLOTS, 2, PIECE, width), dtype),
    ]


def blocks(count, body):
    def step(i, carry):
        body(i)
        return carry

    lax.fori_loop(0, count, step, 0)


def own_tile(k):
    x, y = plane()
    z, core = column()
    return (1 - core) * (z * SIDE + ring(x, -k)) + core * (ring(y, -k) * SIDE + z)


ALL = 2 * SIDE * PIECE


def step_kernel(
    scale,
    x,
    enc_in,
    dec_in,
    enc_bias,
    dec_bias,
    mask,
    sq,
    xs,
    es,
    feat_out,
    grad_out,
    sq_sum,
    enc,
    dec,
    held,
    err,
    feats,
    grads,
    r1,
    r2,
    r4,
    r5,
    norm,
    sq_a,
    sq_b,
    *rest,
):
    fwd, bwd, (local, send, recv) = rest[:5], rest[5:10], rest[10:]
    wires = Wires(send, recv)
    z, core = column()
    flows = [Flow(h) for h in FLOWS]
    slab_count, depth, block = enc.shape
    width = dec.shape[0]
    cols = 512
    loads = [
        pltpu.make_async_copy(enc_in, enc, local.at[18]),
        pltpu.make_async_copy(dec_in, dec, local.at[19]),
    ]
    keep = [pltpu.make_async_copy(x.at[f.h], held.at[0, f.unit(0)], local.at[f.h]) for f in flows]
    saves = {}

    def save(name, k, src, dst):
        n = 2 + len(saves)
        saves[name, k] = pltpu.make_async_copy(src.at[k], dst.at[k], local.at[n])
        saves[name, k].start()

    for copy in keep:
        copy.start()
    for copy in loads:
        copy.start()
    greet()


    def feature(k, e, me, total):
        live = mask[own_tile(k)] > 0.0
        return jnp.where(live, jnp.maximum(total + enc_bias[...], 0.0), 0.0)

    def encode(k, e):
        n = ORDER.index((k, e)) % SLOTS
        if (k, e) == ORDER[0]:
            for copy in keep + loads:
                copy.wait()

        def step(slab):
            rows = held[k, :, piece(e)].reshape(ALL, depth)
            at = pl.ds(pl.multiple_of(slab * block, block), block)
            value = jnp.dot(rows, enc[slab], preferred_element_type=F32)
            fwd[0][n, :, :, at] = value.reshape(2 * SIDE, PIECE, block)

        blocks(slab_count, step)
        if e == PIECES[-1]:
            save("x", k, held, xs)

    swap = wires.copy("sq", sq, sq_a.at[0], tok_peer(z, 1 - core))
    turns = [wires.copy(("sq", d), sq_b.at[0], sq_b.at[1 + s(d)], tok_peer(ring(z, d), core)) for d in DIRS]
    turn_on = wires.copy(("sq", 2), sq_b.at[1], sq_b.at[3], tok_peer(ring(z, 1), core))

    def norms(stage):
        if stage == 0:
            swap.wait_recv()
            sq_b[0] = sq[...] + sq_a[0]
            for copy in turns:
                wires.go(copy)
        elif stage == 1:
            for copy in turns:
                copy.wait_recv()
            wires.go(turn_on)
        else:
            turn_on.wait_recv()
            total = (sq_b[0] + sq_b[3]) + (sq_b[1] + sq_b[2])
            sq_sum[...] = total
            norm[...] = jnp.sum(jnp.sqrt(total + NORM_EPSILON), axis=0, keepdims=True)

    wires.go(swap)


    ready = set()

    def decode(k, e):
        if k not in ready:
            ready.add(k)
            wires.settle(front.name(k))
            saves["x", k].wait()

        def step(col):
            at = pl.ds(pl.multiple_of(col * cols, cols), cols)
            f = feats[k, :, piece(e)].reshape(ALL, width)
            value = jnp.dot(f, dec[:, at], preferred_element_type=F32)
            held[k, :, piece(e), at] = value.reshape(2 * SIDE, PIECE, cols).astype(BF16)

        blocks(depth // cols, step)

    def half(d, e):
        return pl.ds(e * HALF, HALF)

    def far(f, k, e, d):
        src = held.at[k, f.unit(2), rows_of(d, e)]
        return wires.copy((0, f.h, k, e, d), src, r1.at[f.h, k, s(d), half(d, e)], f.near(0, d))

    def plain(f, k, e, d):
        src = held.at[k, f.unit(d), rows_of(-d, e)]
        return wires.copy((1, f.h, k, e, d), src, r2.at[f.h, k, s(d), rows_of(-d, e)], f.near(0, d))

    def summed(f, k, e, d):
        src = held.at[k, f.unit(d), rows_of(d, e)]
        return wires.copy((2, f.h, k, e, d), src, r2.at[f.h, k, s(d), rows_of(d, e)], f.near(0, d))

    def far2(f, e, d):
        src = held.at[2, f.unit(0), rows_of(d, e)]
        return wires.copy((3, f.h, e, d), src, r4.at[f.h, s(d), half(d, e)], f.near(d, 0))

    def plain2(f, e, d):
        src = held.at[3 if d == 1 else 1, f.unit(0), rows_of(-d, e)]
        return wires.copy((4, f.h, e, d), src, r5.at[f.h, s(d), rows_of(-d, e)], f.near(d, 0))

    def summed2(f, e, d):
        src = held.at[3 if d == 1 else 1, f.unit(0), rows_of(d, e)]
        return wires.copy((5, f.h, e, d), src, r5.at[f.h, s(d), rows_of(d, e)], f.near(d, 0))

    def reduce_begin(k, e):
        decode(k, e)
        for make in (far, plain):
            for f in flows:
                for d in DIRS:
                    wires.go(make(f, k, e, d))

    def reduce_relay(k, e):
        for f in flows:
            for d in DIRS:
                far(f, k, e, d).wait_recv()
                at = (k, f.unit(d), rows_of(d, e))
                held[at] = (f32(held[at]) + f32(r1[f.h, k, s(d), half(d, e)])).astype(BF16)
                wires.go(summed(f, k, e, d))

    def reduce(k, e):
        for f in flows:
            for d in DIRS:
                plain(f, k, e, d).wait_recv()
                summed(f, k, e, d).wait_recv()
            at = (k, f.unit(0), piece(e))
            total = f32(held[at]) + f32(r2[f.h, k, 0, piece(e)]) + f32(r2[f.h, k, 1, piece(e)])
            held[at] = total.astype(BF16)
            if k == 2:
                for d in DIRS:
                    wires.go(far2(f, e, d))
            elif k != 0:
                wires.go(plain2(f, e, 1 if k == 3 else -1))

    def reduce_far(e):
        for f in flows:
            for d in DIRS:
                far2(f, e, d).wait_recv()
                at = (3 if d == 1 else 1, f.unit(0), rows_of(d, e))
                held[at] = (f32(held[at]) + f32(r4[f.h, s(d), half(d, e)])).astype(BF16)
                wires.go(summed2(f, e, d))

    def finish(e):
        for f in flows:
            for d in DIRS:
                plain2(f, e, d).wait_recv()
                summed2(f, e, d).wait_recv()
            at = f.unit(0), piece(e)
            recon = f32(held[(0,) + at]) + f32(r5[f.h, 0, piece(e)]) + f32(r5[f.h, 1, piece(e)]) + dec_bias[...]
            err[(0,) + at] = (recon - f32(x[f.h, piece(e)])).astype(BF16)
        if e == PIECES[-1]:
            wires.drain()


    def project(k, e):
        n = ORDER.index((k, e)) % SLOTS

        def step(slab):
            at = pl.ds(pl.multiple_of(slab * block, block), block)
            rows = err[k, :, piece(e)].reshape(ALL, depth)
            value = lax.dot_general(rows, dec[at], NT, preferred_element_type=F32)
            bwd[0][n, :, :, at] = value.reshape(2 * SIDE, PIECE, block).astype(BF16)

        blocks(slab_count, step)
        if e == PIECES[-1]:
            save("e", k, err, es)

    def pre_grad(k, e, me, total):
        grad = scale * (total + SPARSITY * norm[...])
        return jnp.where(f32(feats[k, me, piece(e)]) > 0.0, grad, 0.0)

    front = Gather(wires, flows, "x", lambda h, e: x.at[h, piece(e)], held)
    back = Gather(wires, flows, "e", lambda h, e: err.at[0, flows[h].unit(0), piece(e)], err)
    toks = {
        FWD: {g: tok_flow(wires, FWD, *g, fwd[0], feats, *fwd[1:], feature) for g in ORDER},
        BWD: {g: tok_flow(wires, BWD, *g, bwd[0], grads, *bwd[1:], pre_grad) for g in ORDER},
    }

    done = []

    def tok(phase, k, e, number):
        next(toks[phase][k, e])
        done.append((phase, k, number))
        if number == 7 and done.count((phase, k, 7)) == len(PIECES):
            save(phase, k, *((feats, feat_out) if phase == FWD else (grads, grad_out)))

    steps = {MID: {BEGIN: reduce_begin, RELAY: reduce_relay, REDUCE: reduce, JOIN: reduce_far, FINISH: finish}}
    for phase, g, work in ((FWD, front, encode), (BWD, back, project)):
        steps[phase] = {SEND: g.send, CROSS: g.cross, NEAR: g.near, FAR: g.far, RELAY: g.relay, NORM: norms}
        steps[phase][TOK] = functools.partial(tok, phase)

        def arrive(k, e, g=g, work=work):
            g.complete(k, e)
            work(k, e)

        steps[phase][WORK] = arrive
    for phase, what, *where in SCRIPT:
        steps[phase][what](*where)
    for (name, _), copy in saves.items():
        if name != "x":
            copy.wait()
    wires.drain()


VMEM = pl.BlockSpec(memory_space=pltpu.VMEM)
ANY = pl.BlockSpec(memory_space=pl.ANY)


def step(scale, x, enc, dec, enc_bias, dec_bias, mask, sq):
    width, depth = dec.shape
    units = (SIDE, 2 * SIDE, UNIT)
    rows = jax.ShapeDtypeStruct(units + (depth,), BF16)
    latents = jax.ShapeDtypeStruct(units + (width,), BF16)
    return pl.pallas_call(
        functools.partial(step_kernel, scale),
        out_shape=[rows, rows, latents, latents, jax.ShapeDtypeStruct(sq.shape, F32)],
        in_specs=[VMEM, ANY, ANY] + [VMEM] * 4,
        out_specs=[ANY, ANY, ANY, ANY, VMEM],
        scratch_shapes=[
            pltpu.VMEM(enc.shape, BF16),
            pltpu.VMEM(dec.shape, BF16),
            pltpu.VMEM(units + (depth,), BF16),
            pltpu.VMEM(units + (depth,), BF16),
            pltpu.VMEM(units + (width,), BF16),
            pltpu.VMEM(units + (width,), BF16),
            pltpu.VMEM((2, SIDE, 2, UNIT // 2, depth), BF16),
            pltpu.VMEM((2, SIDE, 2, UNIT, depth), BF16),
            pltpu.VMEM((2, 2, UNIT // 2, depth), BF16),
            pltpu.VMEM((2, 2, UNIT, depth), BF16),
            pltpu.VMEM((1, width), F32),
            pltpu.VMEM((1,) + sq.shape, F32),
            pltpu.VMEM((4,) + sq.shape, F32),
        ]
        + tok_buffers(F32, width)
        + tok_buffers(BF16, width)
        + [
            pltpu.SemaphoreType.DMA((20,)),
            pltpu.SemaphoreType.DMA((348,)),
            pltpu.SemaphoreType.DMA((348,)),
        ],
        compiler_params=pltpu.CompilerParams(
            vmem_limit_bytes=60 * 1024 * 1024, collective_id=0, has_side_effects=True
        ),
        name="step",
    )(x, enc, dec, enc_bias, dec_bias, mask, sq)


QUAD = 8


def weights_kernel(
    scale, units, count, xs, es, feats, grads, dec, inv_norm, grad_enc, grad_dec, enc_sum, err_sum, acc_e, acc_d, tot, gsum, mixed
):
    slab = pl.program_id(0)
    models, part = grad_enc.shape[1], grad_enc.shape[2]
    cols = err_sum.shape[2]
    rows = es[:, :, pl.ds(pl.multiple_of(slab * cols, cols), cols)].reshape(-1, cols)
    err_sum[0] = scale * jnp.dot(jnp.ones((16, rows.shape[0]), BF16), rows, preferred_element_type=F32)[:8]
    acc_e[...] = jnp.zeros_like(acc_e)
    acc_d[...] = jnp.zeros_like(acc_d)
    tot[...] = jnp.zeros_like(tot)
    gsum[...] = jnp.zeros_like(gsum)

    def pair(i, carry):
        ids = [units[slab * 2 * MOST + i * QUAD + n] for n in range(QUAD)]
        f = jnp.concatenate([feats[n] for n in ids], axis=0)
        g = jnp.concatenate([grads[n] for n in ids], axis=0)
        a = jnp.concatenate([xs[n] for n in ids], axis=0)
        e = jnp.concatenate([es[n] for n in ids], axis=0)
        acc_e[...] += lax.dot_general(g, a, TN, preferred_element_type=F32)
        acc_d[...] += lax.dot_general(f, e, TN, preferred_element_type=F32)
        tot[...] += lax.dot_general(f, jnp.ones((QUAD * UNIT, 128), BF16), TN, preferred_element_type=F32)
        gsum[...] += jnp.dot(jnp.ones((16, QUAD * UNIT), BF16), g, preferred_element_type=F32)
        return carry

    lax.fori_loop(0, lax.div(count[slab] + 3, 4), pair, 0)
    enc_sum[...] = gsum[:8]
    for m in range(models):
        at = pl.ds(m * part, part)
        grad_enc[0, m] = acc_e[:, at].astype(BF16).T
        col = SPARSITY * tot[:, :1] * inv_norm[m]
        mixed[:, m, :] = scale * (acc_d[:, at] + col * f32(dec[:, at]))
    grad_dec[...] = mixed[...].astype(grad_dec.dtype)


def weights(scale, units, count, xs, es, feats, grads, dec, inv_norm, models, slabs):
    width, depth = dec.shape
    block = width // slabs
    part = depth // models
    cols = depth // slabs
    once = pl.Buffered(1)

    def whole(a):
        return pl.BlockSpec(a.shape, lambda c, *_: (0,) * a.ndim, pipeline_mode=once)

    return pl.pallas_call(
        functools.partial(weights_kernel, scale),
        out_shape=[
            jax.ShapeDtypeStruct((slabs, models, part, block), BF16),
            jax.ShapeDtypeStruct((width, models, part), BF16),
            jax.ShapeDtypeStruct((8, width), F32),
            jax.ShapeDtypeStruct((slabs, 8, cols), F32),
        ],
        grid_spec=pltpu.PrefetchScalarGridSpec(
            num_scalar_prefetch=2,
            grid=(slabs,),
            in_specs=[
                whole(xs),
                whole(es),
                pl.BlockSpec(feats.shape[:2] + (block,), lambda c, *_: (0, 0, c)),
                pl.BlockSpec(grads.shape[:2] + (block,), lambda c, *_: (0, 0, c)),
                pl.BlockSpec((block, depth), lambda c, *_: (c, 0)),
                pl.BlockSpec((models, block, 1), lambda c, *_: (0, c, 0)),
            ],
            out_specs=[
                pl.BlockSpec((1, models, part, block), lambda c, *_: (c, 0, 0, 0)),
                pl.BlockSpec((block, models, part), lambda c, *_: (c, 0, 0)),
                pl.BlockSpec((8, block), lambda c, *_: (0, c)),
                pl.BlockSpec((1, 8, cols), lambda c, *_: (c, 0, 0)),
            ],
            scratch_shapes=[
                pltpu.VMEM((block, depth), F32),
                pltpu.VMEM((block, depth), F32),
                pltpu.VMEM((block, 128), F32),
                pltpu.VMEM((16, block), F32),
                pltpu.VMEM((block, models, part), F32),
            ],
        ),
        compiler_params=pltpu.CompilerParams(vmem_limit_bytes=56 * 1024 * 1024),
        name="weights",
    )(units, count, xs, es, feats, grads, dec, inv_norm)


def unit_lists(is_active):
    tiles = is_active.shape[0]
    ids = jnp.arange(tiles, dtype=jnp.int32)
    before = (ids[:, None] > ids[None, :]).astype(jnp.int32)
    rank = jnp.sum(before[:, :, None] * is_active[None], axis=1)
    places = jnp.arange(MOST, dtype=jnp.int32)
    picked = (is_active[:, :, None] == 1) & (rank[:, :, None] == places)
    idle = jnp.min(jnp.where(is_active == 0, ids[:, None], tiles - 1), axis=0)
    count = jnp.sum(is_active, axis=0)
    tile = jnp.sum(jnp.where(picked, ids[:, None, None], 0), axis=0)
    tile = jnp.where(places[None, :] < count[:, None], tile, idle[:, None])
    x, y = plane()
    tx, ty = tile % SIDE, tile // SIDE
    one = ((x - tx) % SIDE) * 2 * SIDE + ty
    two = ((y - ty) % SIDE) * 2 * SIDE + SIDE + tx
    return jnp.stack([one, two], axis=2).reshape(-1), count


def on_device(activations, enc_weight, enc_bias, dec_weight, dec_bias, active):
    slabs, models, depth, block = enc_weight.shape
    rows, tiles = activations.shape[0], active.shape[0]
    width = slabs * block
    scale = 1.0 / math.sqrt(MOST * TILE)
    ids = lax.axis_index("lat") * slabs + jnp.arange(slabs, dtype=jnp.int32)
    is_active = jnp.any(active[:, :, None] == ids[None, None, :], axis=1).astype(jnp.int32)
    mask = jnp.broadcast_to(is_active.astype(F32)[:, None, :, None], (tiles, 1, slabs, block))
    mask = mask.reshape(tiles, 1, width)
    units, count = unit_lists(is_active)
    x = activations.reshape(2, rows // 2, models * depth)
    dec = dec_weight.reshape(width, models * depth)
    sq = jnp.stack(
        [jnp.sum(jnp.square(dec[:, m * depth : (m + 1) * depth].astype(F32)), axis=1) for m in range(models)]
    )
    enc = enc_weight.reshape(slabs, models * depth, block)
    xs, es, feats, grads, sq_sum = step(
        scale, x, enc, dec, enc_bias.reshape(1, width), dec_bias.reshape(1, models * depth), mask, sq
    )
    inv_norm = (1.0 / jnp.sqrt(sq_sum + NORM_EPSILON))[:, :, None]
    flat = (2 * tiles, UNIT)
    grad_enc, grad_dec, enc_sum, err_sum = weights(
        scale,
        units,
        count,
        xs.reshape(flat + (models * depth,)),
        es.reshape(flat + (models * depth,)),
        feats.reshape(flat + (width,)),
        grads.reshape(flat + (width,)),
        dec,
        inv_norm,
        models,
        slabs,
    )
    return (
        grad_enc,
        enc_sum[0].reshape(slabs, block),
        grad_dec.reshape(dec_weight.shape),
        err_sum[:, 0].reshape(models, depth),
    )


def solution(mesh):
    placed = (
        P("lat", None, "tok"),
        P("lat", None, "tok", None),
        P("lat", None),
        P("lat", None, None, "tok"),
        P(None, "tok"),
        P(),
    )
    return jax.shard_map(
        on_device,
        mesh=mesh,
        in_specs=placed,
        out_specs=(
            P("lat", None, "tok", None),
            P("lat", None),
            P("lat", None, None, "tok"),
            P(None, "tok"),
        ),
        check_vma=False,
    )
```

```python
import functools
import math

import jax
import jax.numpy as jnp
from jax import lax
from jax.experimental import pallas as pl
from jax.experimental.pallas import tpu as pltpu
from jax.sharding import PartitionSpec as P

MOST = 8
TILE = 128
SPARSITY = 0.25
NORM_EPSILON = 1e-06
MESH = pl.DeviceIdType.MESH
SIDE = 4
UNIT = TILE // 2
PIECE = UNIT // 2
HALF = PIECE // 2
PIECES = (0, 1)
SLOTS = 4
DIRS = (1, -1)
ORDER = tuple((k, e) for k in (0, 1, 3, 2) for e in PIECES)
BF16, F32 = jnp.bfloat16, jnp.float32
NT = (((1,), (1,)), ((), ()))
TN = (((0,), (0,)), ((), ()))


def ring(i, step):
    return lax.rem(i + step + SIDE, SIDE)


def lat_peer(y, x):
    return {"lat": y * SIDE + x}


def tok_peer(z, core):
    return {"tok": z * 2 + core}


def plane():
    lat = lax.axis_index("lat")
    return lax.rem(lat, SIDE), lax.div(lat, SIDE)


def column():
    tok = lax.axis_index("tok")
    return lax.div(tok, 2), lax.rem(tok, 2)


def greet():
    x, y = plane()
    z, core = column()
    peers = [lat_peer(y, ring(x, d)) for d in DIRS] + [lat_peer(ring(y, d), x) for d in DIRS]
    peers += [tok_peer(ring(z, d), core) for d in DIRS] + [tok_peer(z, 1 - core)]
    barrier = pltpu.get_barrier_semaphore()
    for peer in peers:
        pl.semaphore_signal(barrier, inc=1, device_id=peer, device_id_type=MESH)
    pl.semaphore_wait(barrier, len(peers))


def s(d):
    return 0 if d == 1 else 1


def rows_of(d, e=0):
    return pl.ds(e * PIECE + (0 if d == 1 else HALF), HALF)


def piece(e):
    return pl.ds(e * PIECE, PIECE)


def f32(v):
    return v.astype(F32)


class Wires:
    def __init__(self, send, recv):
        self.send, self.recv = send, recv
        self.numbers, self.started = {}, []

    def copy(self, key, src, dst, peer):
        n = self.numbers.setdefault(key, len(self.numbers))
        return pltpu.make_async_remote_copy(
            src_ref=src,
            dst_ref=dst,
            send_sem=self.send.at[n],
            recv_sem=self.recv.at[n],
            device_id=peer,
            device_id_type=MESH,
        )

    def go(self, copy, source=None):
        copy.start()
        self.started.append((source, copy))

    def settle(self, source):
        for name, copy in self.started:
            if name == source:
                copy.wait_send()
        self.started = [item for item in self.started if item[0] != source]

    def drain(self):
        for _, copy in self.started:
            copy.wait_send()
        self.started = []


FLOWS = (0, 1)
FWD, MID, BWD = range(3)
SEND, CROSS, NEAR, FAR, RELAY, WORK, TOK, NORM, BEGIN, REDUCE, JOIN, FINISH = range(12)
SCRIPT = (
    (FWD, SEND, 0, 0), (FWD, CROSS, 0), (FWD, SEND, 0, 1), (FWD, RELAY, 0, 0), (FWD, CROSS, 1),
    (FWD, NEAR, 0), (FWD, RELAY, 0, 1), (FWD, WORK, 0, 0), (FWD, TOK, 0, 0, 1), (FWD, NORM, 0),
    (FWD, SEND, 1, 0), (FWD, NEAR, 1), (FWD, FAR, 0), (FWD, TOK, 0, 0, 2), (FWD, WORK, 0, 1),
    (FWD, TOK, 0, 1, 1), (FWD, SEND, 1, 1), (FWD, RELAY, 1, 0), (FWD, TOK, 0, 0, 3), (FWD, FAR, 1),
    (FWD, SEND, 3, 0), (FWD, TOK, 0, 1, 2), (FWD, TOK, 0, 0, 4), (FWD, RELAY, 1, 1),
    (FWD, WORK, 1, 0), (FWD, NORM, 1), (FWD, TOK, 0, 1, 3), (FWD, TOK, 1, 0, 1), (FWD, RELAY, 3, 0),
    (FWD, TOK, 0, 0, 5), (FWD, WORK, 1, 1), (FWD, TOK, 0, 1, 4), (FWD, TOK, 1, 1, 1),
    (FWD, TOK, 1, 0, 2), (FWD, TOK, 0, 0, 6), (FWD, SEND, 3, 1), (FWD, SEND, 2, 0), (FWD, WORK, 3, 0),
    (FWD, NORM, 2), (FWD, TOK, 3, 0, 1), (FWD, TOK, 0, 1, 5), (FWD, TOK, 1, 1, 2),
    (FWD, TOK, 1, 0, 3), (FWD, TOK, 0, 0, 7), (FWD, RELAY, 3, 1), (FWD, TOK, 0, 1, 6),
    (FWD, TOK, 3, 0, 2), (FWD, SEND, 2, 1), (FWD, TOK, 1, 1, 3), (FWD, TOK, 0, 1, 7),
    (FWD, RELAY, 2, 0), (FWD, WORK, 3, 1), (FWD, TOK, 3, 1, 1), (FWD, TOK, 1, 0, 4),
    (FWD, TOK, 3, 0, 3), (FWD, RELAY, 2, 1), (FWD, TOK, 1, 1, 4), (FWD, TOK, 3, 1, 2),
    (FWD, TOK, 1, 0, 5), (FWD, WORK, 2, 0), (FWD, TOK, 2, 0, 1), (FWD, TOK, 3, 0, 4),
    (FWD, TOK, 1, 1, 5), (FWD, WORK, 2, 1), (MID, BEGIN, 0, 1), (FWD, TOK, 3, 1, 3),
    (FWD, TOK, 2, 0, 2), (FWD, TOK, 1, 0, 6), (MID, BEGIN, 0, 0), (FWD, TOK, 3, 0, 5),
    (FWD, TOK, 1, 1, 6), (MID, RELAY, 0, 1), (FWD, TOK, 2, 1, 1), (FWD, TOK, 1, 0, 7),
    (MID, BEGIN, 1, 0), (FWD, TOK, 2, 0, 3), (FWD, TOK, 1, 1, 7), (MID, BEGIN, 1, 1),
    (FWD, TOK, 3, 0, 6), (FWD, TOK, 2, 1, 2), (MID, RELAY, 0, 0), (MID, REDUCE, 0, 1),
    (FWD, TOK, 3, 0, 7), (FWD, TOK, 2, 0, 4), (MID, RELAY, 1, 0), (MID, BEGIN, 3, 0),
    (FWD, TOK, 2, 1, 3), (MID, RELAY, 1, 1), (FWD, TOK, 3, 1, 4), (FWD, TOK, 2, 0, 5),
    (MID, REDUCE, 0, 0), (FWD, TOK, 2, 1, 4), (MID, REDUCE, 1, 0), (FWD, TOK, 3, 1, 5),
    (FWD, TOK, 2, 0, 6), (MID, RELAY, 3, 0), (FWD, TOK, 2, 1, 5), (FWD, TOK, 2, 0, 7),
    (MID, BEGIN, 2, 0), (MID, REDUCE, 1, 1), (FWD, TOK, 2, 1, 6), (FWD, TOK, 3, 1, 6),
    (MID, REDUCE, 3, 0), (FWD, TOK, 2, 1, 7), (MID, BEGIN, 2, 1), (FWD, TOK, 3, 1, 7),
    (MID, RELAY, 2, 0), (MID, BEGIN, 3, 1), (MID, RELAY, 2, 1), (MID, REDUCE, 2, 0),
    (MID, RELAY, 3, 1), (MID, REDUCE, 2, 1), (MID, JOIN, 0), (MID, REDUCE, 3, 1), (MID, JOIN, 1),
    (MID, FINISH, 0), (BWD, SEND, 0, 0), (BWD, CROSS, 0), (MID, FINISH, 1), (BWD, SEND, 0, 1),
    (BWD, RELAY, 0, 0), (BWD, NEAR, 0), (BWD, SEND, 1, 0), (BWD, RELAY, 0, 1), (BWD, WORK, 0, 0),
    (BWD, TOK, 0, 0, 1), (BWD, FAR, 0), (BWD, CROSS, 1), (BWD, TOK, 0, 0, 2), (BWD, RELAY, 1, 0),
    (BWD, WORK, 0, 1), (BWD, TOK, 0, 1, 1), (BWD, TOK, 0, 0, 3), (BWD, NEAR, 1), (BWD, SEND, 1, 1),
    (BWD, TOK, 0, 1, 2), (BWD, TOK, 0, 0, 4), (BWD, WORK, 1, 0), (BWD, TOK, 1, 0, 1), (BWD, FAR, 1),
    (BWD, SEND, 3, 0), (BWD, TOK, 0, 1, 3), (BWD, RELAY, 1, 1), (BWD, TOK, 1, 0, 2),
    (BWD, TOK, 0, 1, 4), (BWD, TOK, 0, 0, 5), (BWD, SEND, 3, 1), (BWD, RELAY, 3, 0),
    (BWD, TOK, 1, 0, 3), (BWD, WORK, 1, 1), (BWD, TOK, 1, 1, 1), (BWD, TOK, 0, 1, 5),
    (BWD, SEND, 2, 0), (BWD, TOK, 0, 0, 6), (BWD, RELAY, 3, 1), (BWD, TOK, 1, 0, 4),
    (BWD, TOK, 1, 1, 2), (BWD, TOK, 0, 0, 7), (BWD, TOK, 0, 1, 6), (BWD, WORK, 3, 0),
    (BWD, SEND, 2, 1), (BWD, TOK, 3, 0, 1), (BWD, TOK, 1, 0, 5), (BWD, RELAY, 2, 0),
    (BWD, TOK, 0, 1, 7), (BWD, TOK, 1, 1, 3), (BWD, WORK, 3, 1), (BWD, TOK, 3, 0, 2),
    (BWD, TOK, 1, 0, 6), (BWD, TOK, 1, 1, 4), (BWD, TOK, 3, 1, 1), (BWD, RELAY, 2, 1),
    (BWD, TOK, 1, 0, 7), (BWD, WORK, 2, 0), (BWD, TOK, 3, 0, 3), (BWD, TOK, 2, 0, 1),
    (BWD, TOK, 3, 1, 2), (BWD, TOK, 1, 1, 5), (BWD, WORK, 2, 1), (BWD, TOK, 2, 1, 1),
    (BWD, TOK, 3, 0, 4), (BWD, TOK, 2, 0, 2), (BWD, TOK, 3, 1, 3), (BWD, TOK, 1, 1, 6),
    (BWD, TOK, 2, 1, 2), (BWD, TOK, 3, 0, 5), (BWD, TOK, 2, 0, 3), (BWD, TOK, 1, 1, 7),
    (BWD, TOK, 3, 1, 4), (BWD, TOK, 2, 1, 3), (BWD, TOK, 3, 0, 6), (BWD, TOK, 2, 0, 4),
    (BWD, TOK, 3, 1, 5), (BWD, TOK, 3, 0, 7), (BWD, TOK, 2, 1, 4), (BWD, TOK, 2, 0, 5),
    (BWD, TOK, 3, 1, 6), (BWD, TOK, 2, 1, 5), (BWD, TOK, 2, 0, 6), (BWD, TOK, 3, 1, 7),
    (BWD, TOK, 2, 1, 6), (BWD, TOK, 2, 0, 7), (BWD, TOK, 2, 1, 7),
)


class Flow:
    def __init__(self, h):
        x, y = plane()
        self.h = h
        self.p, self.q = (x, y) if h == 0 else (y, x)

    def near(self, dp, dq):
        p, q = ring(self.p, dp), ring(self.q, dq)
        return lat_peer(q, p) if self.h == 0 else lat_peer(p, q)

    def unit(self, dq):
        return self.h * SIDE + ring(self.q, dq)


class Gather:
    def __init__(self, wires, flows, tag, own, held):
        self.wires, self.flows, self.tag, self.own, self.held = wires, flows, tag, own, held

    def p1(self, f, e, d):
        dst = self.held.at[1 if d == 1 else 3, f.unit(0), piece(e)]
        return self.wires.copy(("p1", f.h, e, d), self.own(f.h, e), dst, f.near(d, 0))

    def p1half(self, f, e, d):
        src = self.held.at[1 if d == 1 else 3, f.unit(0), rows_of(d, e)]
        dst = self.held.at[2, f.unit(0), rows_of(d, e)]
        return self.wires.copy(("p1half", f.h, e, d), src, dst, f.near(d, 0))

    def p2(self, f, k, e, d):
        at = self.held.at[k, f.unit(0), piece(e)]
        return self.wires.copy(("p2", f.h, k, e, d), self.own(f.h, e) if k == 0 else at, at, f.near(0, d))

    def p2half(self, f, k, e, d):
        at = self.held.at[k, f.unit(-d), rows_of(d, e)]
        return self.wires.copy(("p2half", f.h, k, e, d), at, at, f.near(0, d))

    def name(self, k):
        return (self.tag, k)

    def each(self, make, *where):
        for f in self.flows:
            for d in DIRS:
                yield make(f, *where, d)

    def send(self, k, e):
        for copy in self.each(self.p2, k, e):
            self.wires.go(copy, self.name(k))

    def cross(self, e):
        for copy in self.each(self.p1, e):
            self.wires.go(copy, self.name(0))

    def near(self, e):
        for copy in self.each(self.p1, e):
            copy.wait_recv()
        for f in self.flows:
            for d, k in ((1, 1), (-1, 3)):
                self.wires.go(self.p1half(f, e, d), self.name(k))

    def far(self, e):
        for copy in self.each(self.p1half, e):
            copy.wait_recv()

    def relay(self, k, e):
        for f in self.flows:
            for d in DIRS:
                self.p2(f, k, e, d).wait_recv()
                self.wires.go(self.p2half(f, k, e, d), self.name(k))

    def complete(self, k, e):
        for copy in self.each(self.p2half, k, e):
            copy.wait_recv()


def tok_flow(wires, tag, k, e, part, out, r1, s1, r2, r3, epilogue):
    n = ORDER.index((k, e)) % SLOTS
    z, core = column()
    other = tok_peer(z, 1 - core)
    me = core * SIDE + z
    source = (tag, k, e)

    def peer(d):
        return tok_peer(ring(z, d), core)

    def swap(j):
        at = ring(z, j)
        return wires.copy(("tok", k, e, 0, j), part.at[n, (1 - core) * SIDE + at], r1.at[n, j], other)

    def far(d):
        return wires.copy(("tok", k, e, 1, d), s1.at[n, 2, rows_of(d)], r2.at[n, s(d)], peer(d))

    def plain(d):
        src = s1.at[n, 1 if d == 1 else 3, rows_of(-d)]
        return wires.copy(("tok", k, e, 2, d), src, r3.at[n, s(d), rows_of(-d)], peer(d))

    def summed(d):
        src = s1.at[n, 1 if d == 1 else 3, rows_of(d)]
        return wires.copy(("tok", k, e, 3, d), src, r3.at[n, s(d), rows_of(d)], peer(d))

    def spread(d):
        at = out.at[k, me, piece(e)]
        return wires.copy(("tok", k, e, 4, d), at, at, peer(d))

    def forward(d):
        at = out.at[k, core * SIDE + ring(z, -d), rows_of(d, e)]
        return wires.copy(("tok", k, e, 5, d), at, at, peer(d))

    def hand(j):
        at = out.at[k, core * SIDE + ring(z, j), piece(e)]
        return wires.copy(("tok", k, e, 6, j), at, at, other)

    def first(j):
        swap(j).wait_recv()
        at = core * SIDE + ring(z, j)
        s1[n, j] = (f32(part[n, at]) + f32(r1[n, j])).astype(s1.dtype)

    for j in (2, 1, 3, 0):
        wires.go(swap(j), source)
    yield
    first(2)
    for d in DIRS:
        wires.go(far(d), source)
    for d in DIRS:
        first(1 if d == 1 else 3)
        wires.go(plain(d), source)
    first(0)
    yield
    for d in DIRS:
        far(d).wait_recv()
        j = 1 if d == 1 else 3
        s1[n, j, rows_of(d)] = (f32(s1[n, j, rows_of(d)]) + f32(r2[n, s(d)])).astype(s1.dtype)
        wires.go(summed(d), source)
    yield
    for d in DIRS:
        plain(d).wait_recv()
        summed(d).wait_recv()
    total = f32(s1[n, 0]) + f32(r3[n, 0]) + f32(r3[n, 1])
    out[k, me, piece(e)] = epilogue(k, e, me, total).astype(out.dtype)
    for d in DIRS:
        wires.go(spread(d))
    wires.go(hand(0))
    yield
    for d in DIRS:
        spread(d).wait_recv()
        wires.go(forward(d))
        wires.go(hand(3 if d == 1 else 1))
    hand(0).wait_recv()
    wires.settle(source)
    yield
    for d in DIRS:
        forward(d).wait_recv()
    wires.go(hand(2))
    yield
    for j in range(1, SIDE):
        hand(j).wait_recv()
    yield


def tok_buffers(dtype, width):
    return [
        pltpu.VMEM((SLOTS, 2 * SIDE, PIECE, width), dtype),
        pltpu.VMEM((SLOTS, SIDE, PIECE, width), dtype),
        pltpu.VMEM((SLOTS, SIDE, PIECE, width), dtype),
        pltpu.VMEM((SLOTS, 2, HALF, width), dtype),
        pltpu.VMEM((SLOTS, 2, PIECE, width), dtype),
    ]


def blocks(count, body):
    def step(i, carry):
        body(i)
        return carry

    lax.fori_loop(0, count, step, 0)


def own_tile(k):
    x, y = plane()
    z, core = column()
    return (1 - core) * (z * SIDE + ring(x, -k)) + core * (ring(y, -k) * SIDE + z)


ALL = 2 * SIDE * PIECE


def step_kernel(
    scale,
    x,
    enc_in,
    dec_in,
    enc_rows,
    dec_rows,
    mask,
    sq,
    xs,
    es,
    feat_out,
    grad_out,
    sq_sum,
    enc_bias,
    dec_bias,
    enc,
    dec,
    held,
    err,
    feats,
    grads,
    r1,
    r2,
    r4,
    r5,
    norm,
    sq_a,
    sq_b,
    *rest,
):
    fwd, bwd, (local, send, recv) = rest[:5], rest[5:10], rest[10:]
    wires = Wires(send, recv)
    z, core = column()
    flows = [Flow(h) for h in FLOWS]
    slab_count, depth, block = enc.shape
    width = dec.shape[0]
    cols = 512
    loads = [
        pltpu.make_async_copy(enc_in, enc, local.at[18]),
        pltpu.make_async_copy(dec_in, dec, local.at[19]),
    ]
    keep = [pltpu.make_async_copy(x.at[f.h], held.at[0, f.unit(0)], local.at[f.h]) for f in flows]
    saves = {}

    def save(name, k, src, dst):
        n = 2 + len(saves)
        saves[name, k] = pltpu.make_async_copy(src.at[k], dst.at[k], local.at[n])
        saves[name, k].start()

    for copy in keep:
        copy.start()
    for copy in loads:
        copy.start()
    greet()
    for rows, line in ((enc_rows, enc_bias), (dec_rows, dec_bias)):
        for i in range(rows.shape[0]):
            line[:, pl.ds(i * rows.shape[1], rows.shape[1])] = rows[pl.ds(i, 1)]


    def feature(k, e, me, total):
        live = mask[own_tile(k)] > 0.0
        return jnp.where(live, jnp.maximum(total + enc_bias[...], 0.0), 0.0)

    def encode(k, e):
        n = ORDER.index((k, e)) % SLOTS
        if (k, e) == ORDER[0]:
            for copy in keep + loads:
                copy.wait()

        def step(slab):
            rows = held[k, :, piece(e)].reshape(ALL, depth)
            at = pl.ds(pl.multiple_of(slab * block, block), block)
            value = jnp.dot(rows, enc[slab], preferred_element_type=F32)
            fwd[0][n, :, :, at] = value.reshape(2 * SIDE, PIECE, block)

        blocks(slab_count, step)
        if e == PIECES[-1]:
            save("x", k, held, xs)

    swap = wires.copy("sq", sq, sq_a.at[0], tok_peer(z, 1 - core))
    turns = [wires.copy(("sq", d), sq_b.at[0], sq_b.at[1 + s(d)], tok_peer(ring(z, d), core)) for d in DIRS]
    turn_on = wires.copy(("sq", 2), sq_b.at[1], sq_b.at[3], tok_peer(ring(z, 1), core))

    def norms(stage):
        if stage == 0:
            swap.wait_recv()
            sq_b[0] = sq[...] + sq_a[0]
            for copy in turns:
                wires.go(copy)
        elif stage == 1:
            for copy in turns:
                copy.wait_recv()
            wires.go(turn_on)
        else:
            turn_on.wait_recv()
            total = (sq_b[0] + sq_b[3]) + (sq_b[1] + sq_b[2])
            sq_sum[...] = total
            norm[...] = jnp.sum(jnp.sqrt(total + NORM_EPSILON), axis=0, keepdims=True)

    wires.go(swap)


    ready = set()

    def decode(k, e):
        if k not in ready:
            ready.add(k)
            wires.settle(front.name(k))
            saves["x", k].wait()

        def step(col):
            at = pl.ds(pl.multiple_of(col * cols, cols), cols)
            f = feats[k, :, piece(e)].reshape(ALL, width)
            value = jnp.dot(f, dec[:, at], preferred_element_type=F32)
            held[k, :, piece(e), at] = value.reshape(2 * SIDE, PIECE, cols).astype(BF16)

        blocks(depth // cols, step)

    def half(d, e):
        return pl.ds(e * HALF, HALF)

    def far(f, k, e, d):
        src = held.at[k, f.unit(2), rows_of(d, e)]
        return wires.copy((0, f.h, k, e, d), src, r1.at[f.h, k, s(d), half(d, e)], f.near(0, d))

    def plain(f, k, e, d):
        src = held.at[k, f.unit(d), rows_of(-d, e)]
        return wires.copy((1, f.h, k, e, d), src, r2.at[f.h, k, s(d), rows_of(-d, e)], f.near(0, d))

    def summed(f, k, e, d):
        src = held.at[k, f.unit(d), rows_of(d, e)]
        return wires.copy((2, f.h, k, e, d), src, r2.at[f.h, k, s(d), rows_of(d, e)], f.near(0, d))

    def far2(f, e, d):
        src = held.at[2, f.unit(0), rows_of(d, e)]
        return wires.copy((3, f.h, e, d), src, r4.at[f.h, s(d), half(d, e)], f.near(d, 0))

    def plain2(f, e, d):
        src = held.at[3 if d == 1 else 1, f.unit(0), rows_of(-d, e)]
        return wires.copy((4, f.h, e, d), src, r5.at[f.h, s(d), rows_of(-d, e)], f.near(d, 0))

    def summed2(f, e, d):
        src = held.at[3 if d == 1 else 1, f.unit(0), rows_of(d, e)]
        return wires.copy((5, f.h, e, d), src, r5.at[f.h, s(d), rows_of(d, e)], f.near(d, 0))

    def reduce_begin(k, e):
        decode(k, e)
        for make in (far, plain):
            for f in flows:
                for d in DIRS:
                    wires.go(make(f, k, e, d))

    def reduce_relay(k, e):
        for f in flows:
            for d in DIRS:
                far(f, k, e, d).wait_recv()
                at = (k, f.unit(d), rows_of(d, e))
                held[at] = (f32(held[at]) + f32(r1[f.h, k, s(d), half(d, e)])).astype(BF16)
                wires.go(summed(f, k, e, d))

    def reduce(k, e):
        for f in flows:
            for d in DIRS:
                plain(f, k, e, d).wait_recv()
                summed(f, k, e, d).wait_recv()
            at = (k, f.unit(0), piece(e))
            total = f32(held[at]) + f32(r2[f.h, k, 0, piece(e)]) + f32(r2[f.h, k, 1, piece(e)])
            held[at] = total.astype(BF16)
            if k == 2:
                for d in DIRS:
                    wires.go(far2(f, e, d))
            elif k != 0:
                wires.go(plain2(f, e, 1 if k == 3 else -1))

    def reduce_far(e):
        for f in flows:
            for d in DIRS:
                far2(f, e, d).wait_recv()
                at = (3 if d == 1 else 1, f.unit(0), rows_of(d, e))
                held[at] = (f32(held[at]) + f32(r4[f.h, s(d), half(d, e)])).astype(BF16)
                wires.go(summed2(f, e, d))

    def finish(e):
        for f in flows:
            for d in DIRS:
                plain2(f, e, d).wait_recv()
                summed2(f, e, d).wait_recv()
            at = f.unit(0), piece(e)
            recon = f32(held[(0,) + at]) + f32(r5[f.h, 0, piece(e)]) + f32(r5[f.h, 1, piece(e)]) + dec_bias[...]
            err[(0,) + at] = (recon - f32(x[f.h, piece(e)])).astype(BF16)
        if e == PIECES[-1]:
            wires.drain()


    def project(k, e):
        n = ORDER.index((k, e)) % SLOTS

        def step(slab):
            at = pl.ds(pl.multiple_of(slab * block, block), block)
            rows = err[k, :, piece(e)].reshape(ALL, depth)
            value = lax.dot_general(rows, dec[at], NT, preferred_element_type=F32)
            bwd[0][n, :, :, at] = value.reshape(2 * SIDE, PIECE, block).astype(BF16)

        blocks(slab_count, step)
        if e == PIECES[-1]:
            save("e", k, err, es)

    def pre_grad(k, e, me, total):
        grad = scale * (total + SPARSITY * norm[...])
        return jnp.where(f32(feats[k, me, piece(e)]) > 0.0, grad, 0.0)

    front = Gather(wires, flows, "x", lambda h, e: x.at[h, piece(e)], held)
    back = Gather(wires, flows, "e", lambda h, e: err.at[0, flows[h].unit(0), piece(e)], err)
    toks = {
        FWD: {g: tok_flow(wires, FWD, *g, fwd[0], feats, *fwd[1:], feature) for g in ORDER},
        BWD: {g: tok_flow(wires, BWD, *g, bwd[0], grads, *bwd[1:], pre_grad) for g in ORDER},
    }

    done = []

    def tok(phase, k, e, number):
        next(toks[phase][k, e])
        done.append((phase, k, number))
        if number == 7 and done.count((phase, k, 7)) == len(PIECES):
            save(phase, k, *((feats, feat_out) if phase == FWD else (grads, grad_out)))

    steps = {MID: {BEGIN: reduce_begin, RELAY: reduce_relay, REDUCE: reduce, JOIN: reduce_far, FINISH: finish}}
    for phase, g, work in ((FWD, front, encode), (BWD, back, project)):
        steps[phase] = {SEND: g.send, CROSS: g.cross, NEAR: g.near, FAR: g.far, RELAY: g.relay, NORM: norms}
        steps[phase][TOK] = functools.partial(tok, phase)

        def arrive(k, e, g=g, work=work):
            g.complete(k, e)
            work(k, e)

        steps[phase][WORK] = arrive
    for phase, what, *where in SCRIPT:
        steps[phase][what](*where)
    for (name, _), copy in saves.items():
        if name != "x":
            copy.wait()
    wires.drain()


VMEM = pl.BlockSpec(memory_space=pltpu.VMEM)
ANY = pl.BlockSpec(memory_space=pl.ANY)


def step(scale, x, enc, dec, enc_bias, dec_bias, mask, sq):
    width, depth = dec.shape
    units = (SIDE, 2 * SIDE, UNIT)
    rows = jax.ShapeDtypeStruct(units + (depth,), BF16)
    latents = jax.ShapeDtypeStruct(units + (width,), BF16)
    return pl.pallas_call(
        functools.partial(step_kernel, scale),
        out_shape=[rows, rows, latents, latents, jax.ShapeDtypeStruct(sq.shape, F32)],
        in_specs=[VMEM, ANY, ANY] + [VMEM] * 4,
        out_specs=[ANY, ANY, ANY, ANY, VMEM],
        scratch_shapes=[
            pltpu.VMEM((1, width), F32),
            pltpu.VMEM((1, depth), F32),
            pltpu.VMEM(enc.shape, BF16),
            pltpu.VMEM(dec.shape, BF16),
            pltpu.VMEM(units + (depth,), BF16),
            pltpu.VMEM(units + (depth,), BF16),
            pltpu.VMEM(units + (width,), BF16),
            pltpu.VMEM(units + (width,), BF16),
            pltpu.VMEM((2, SIDE, 2, UNIT // 2, depth), BF16),
            pltpu.VMEM((2, SIDE, 2, UNIT, depth), BF16),
            pltpu.VMEM((2, 2, UNIT // 2, depth), BF16),
            pltpu.VMEM((2, 2, UNIT, depth), BF16),
            pltpu.VMEM((1, width), F32),
            pltpu.VMEM((1,) + sq.shape, F32),
            pltpu.VMEM((4,) + sq.shape, F32),
        ]
        + tok_buffers(F32, width)
        + tok_buffers(BF16, width)
        + [
            pltpu.SemaphoreType.DMA((20,)),
            pltpu.SemaphoreType.DMA((348,)),
            pltpu.SemaphoreType.DMA((348,)),
        ],
        compiler_params=pltpu.CompilerParams(
            vmem_limit_bytes=60 * 1024 * 1024, collective_id=0, has_side_effects=True
        ),
        name="step",
    )(x, enc, dec, enc_bias, dec_bias, mask, sq)


QUAD = 8


def weights_kernel(
    scale, units, count, xs, es, feats, grads, dec, inv_norm, grad_enc, grad_dec, enc_sum, err_sum, acc_e, acc_d, tot, gsum, mixed
):
    slab = pl.program_id(0)
    models, part = grad_enc.shape[1], grad_enc.shape[2]
    cols = err_sum.shape[2]
    rows = es[:, :, pl.ds(pl.multiple_of(slab * cols, cols), cols)].reshape(-1, cols)
    err_sum[0] = scale * jnp.dot(jnp.ones((16, rows.shape[0]), BF16), rows, preferred_element_type=F32)[:8]
    acc_e[...] = jnp.zeros_like(acc_e)
    acc_d[...] = jnp.zeros_like(acc_d)
    tot[...] = jnp.zeros_like(tot)
    gsum[...] = jnp.zeros_like(gsum)

    def pair(i, carry):
        ids = [units[slab * 2 * MOST + i * QUAD + n] for n in range(QUAD)]
        f = jnp.concatenate([feats[n] for n in ids], axis=0)
        g = jnp.concatenate([grads[n] for n in ids], axis=0)
        a = jnp.concatenate([xs[n] for n in ids], axis=0)
        e = jnp.concatenate([es[n] for n in ids], axis=0)
        acc_e[...] += lax.dot_general(g, a, TN, preferred_element_type=F32)
        acc_d[...] += lax.dot_general(f, e, TN, preferred_element_type=F32)
        tot[...] += lax.dot_general(f, jnp.ones((QUAD * UNIT, 128), BF16), TN, preferred_element_type=F32)
        gsum[...] += jnp.dot(jnp.ones((16, QUAD * UNIT), BF16), g, preferred_element_type=F32)
        return carry

    lax.fori_loop(0, lax.div(count[slab] + 3, 4), pair, 0)
    enc_sum[...] = gsum[:8]
    for m in range(models):
        at = pl.ds(m * part, part)
        grad_enc[0, m] = acc_e[:, at].astype(BF16).T
        col = SPARSITY * tot[:, :1] * inv_norm[m]
        mixed[:, m, :] = scale * (acc_d[:, at] + col * f32(dec[:, at]))
    grad_dec[...] = mixed[...].astype(grad_dec.dtype)


def weights(scale, units, count, xs, es, feats, grads, dec, inv_norm, models, slabs):
    width, depth = dec.shape
    block = width // slabs
    part = depth // models
    cols = depth // slabs
    once = pl.Buffered(1)

    def whole(a):
        return pl.BlockSpec(a.shape, lambda c, *_: (0,) * a.ndim, pipeline_mode=once)

    return pl.pallas_call(
        functools.partial(weights_kernel, scale),
        out_shape=[
            jax.ShapeDtypeStruct((slabs, models, part, block), BF16),
            jax.ShapeDtypeStruct((width, models, part), BF16),
            jax.ShapeDtypeStruct((8, width), F32),
            jax.ShapeDtypeStruct((slabs, 8, cols), F32),
        ],
        grid_spec=pltpu.PrefetchScalarGridSpec(
            num_scalar_prefetch=2,
            grid=(slabs,),
            in_specs=[
                whole(xs),
                whole(es),
                pl.BlockSpec(feats.shape[:2] + (block,), lambda c, *_: (0, 0, c)),
                pl.BlockSpec(grads.shape[:2] + (block,), lambda c, *_: (0, 0, c)),
                pl.BlockSpec((block, depth), lambda c, *_: (c, 0)),
                pl.BlockSpec((models, block, 1), lambda c, *_: (0, c, 0)),
            ],
            out_specs=[
                pl.BlockSpec((1, models, part, block), lambda c, *_: (c, 0, 0, 0)),
                pl.BlockSpec((block, models, part), lambda c, *_: (c, 0, 0)),
                pl.BlockSpec((8, block), lambda c, *_: (0, c)),
                pl.BlockSpec((1, 8, cols), lambda c, *_: (c, 0, 0)),
            ],
            scratch_shapes=[
                pltpu.VMEM((block, depth), F32),
                pltpu.VMEM((block, depth), F32),
                pltpu.VMEM((block, 128), F32),
                pltpu.VMEM((16, block), F32),
                pltpu.VMEM((block, models, part), F32),
            ],
        ),
        compiler_params=pltpu.CompilerParams(vmem_limit_bytes=56 * 1024 * 1024),
        name="weights",
    )(units, count, xs, es, feats, grads, dec, inv_norm)


def unit_lists(is_active):
    tiles = is_active.shape[0]
    ids = jnp.arange(tiles, dtype=jnp.int32)
    before = (ids[:, None] > ids[None, :]).astype(jnp.int32)
    rank = jnp.sum(before[:, :, None] * is_active[None], axis=1)
    places = jnp.arange(MOST, dtype=jnp.int32)
    picked = (is_active[:, :, None] == 1) & (rank[:, :, None] == places)
    idle = jnp.min(jnp.where(is_active == 0, ids[:, None], tiles - 1), axis=0)
    count = jnp.sum(is_active, axis=0)
    tile = jnp.sum(jnp.where(picked, ids[:, None, None], 0), axis=0)
    tile = jnp.where(places[None, :] < count[:, None], tile, idle[:, None])
    x, y = plane()
    tx, ty = tile % SIDE, tile // SIDE
    one = ((x - tx) % SIDE) * 2 * SIDE + ty
    two = ((y - ty) % SIDE) * 2 * SIDE + SIDE + tx
    return jnp.stack([one, two], axis=2).reshape(-1), count


def on_device(activations, enc_weight, enc_bias, dec_weight, dec_bias, active):
    slabs, models, depth, block = enc_weight.shape
    rows, tiles = activations.shape[0], active.shape[0]
    width = slabs * block
    scale = 1.0 / math.sqrt(MOST * TILE)
    ids = lax.axis_index("lat") * slabs + jnp.arange(slabs, dtype=jnp.int32)
    is_active = jnp.any(active[:, :, None] == ids[None, None, :], axis=1).astype(jnp.int32)
    mask = jnp.broadcast_to(is_active.astype(F32)[:, None, :, None], (tiles, 1, slabs, block))
    mask = mask.reshape(tiles, 1, width)
    units, count = unit_lists(is_active)
    x = activations.reshape(2, rows // 2, models * depth)
    dec = dec_weight.reshape(width, models * depth)
    sq = jnp.stack(
        [jnp.sum(jnp.square(dec[:, m * depth : (m + 1) * depth].astype(F32)), axis=1) for m in range(models)]
    )
    enc = enc_weight.reshape(slabs, models * depth, block)
    xs, es, feats, grads, sq_sum = step(
        scale, x, enc, dec, enc_bias, dec_bias, mask, sq
    )
    inv_norm = (1.0 / jnp.sqrt(sq_sum + NORM_EPSILON))[:, :, None]
    flat = (2 * tiles, UNIT)
    grad_enc, grad_dec, enc_sum, err_sum = weights(
        scale,
        units,
        count,
        xs.reshape(flat + (models * depth,)),
        es.reshape(flat + (models * depth,)),
        feats.reshape(flat + (width,)),
        grads.reshape(flat + (width,)),
        dec,
        inv_norm,
        models,
        slabs,
    )
    return (
        grad_enc,
        enc_sum[0].reshape(slabs, block),
        grad_dec.reshape(dec_weight.shape),
        err_sum[:, 0].reshape(models, depth),
    )


def solution(mesh):
    placed = (
        P("lat", None, "tok"),
        P("lat", None, "tok", None),
        P("lat", None),
        P("lat", None, None, "tok"),
        P(None, "tok"),
        P(),
    )
    return jax.shard_map(
        on_device,
        mesh=mesh,
        in_specs=placed,
        out_specs=(
            P("lat", None, "tok", None),
            P("lat", None),
            P("lat", None, None, "tok"),
            P(None, "tok"),
        ),
        check_vma=False,
    )
```
